128 devices in a mesh: seq: 32 (over y_hi, x, z), head: 4 (over y_lo, core).
Axes of the slice: x: 4, y: 4 (y_hi: 2, y_lo: 2; y = y_hi * 2 + y_lo), z: 4, core: 2. Of those that a mesh axis runs over, the one named last changes fastest.
Arguments:
- queries: bfloat16 [16384, 20, 128], P('seq', 'head'), may hold values from -17 to 17
- key_rows: bfloat16 [16384, 20, 128], P('seq', 'head'), may hold values from -17 to 17
- value_rows: bfloat16 [16384, 20, 128], P('seq', 'head'), may hold values from -6 to 6
- out_weight: bfloat16 [20, 128, 5120], P('head'), may hold values from -0.5 to 0.5
- tile_mask: int32 [128, 128], replicated, may hold values from 0 to 1, as said below
Outputs:
- mixed: bfloat16 [16384, 5120], P('seq', 'head')
The draws below stay inside these ranges and needn't reach their ends.
Inputs may be any that keep to these rules, and one draw needn't show every extreme that they name: tile_mask[a, b] = 1 exactly when tiles a and b lie in the same or adjacent slabs, a slab being 8 consecutive tiles, and their places in the slab's grid of 2 rows by 4 columns differ by at most one row and one column; each slab assigns its 8 tiles to the 8 places of its grid in its own arbitrary order. tile_mask is symmetric with ones on its diagonal, and zero between tokens whose devices along seq are more than 3 apart.
All inputs are finite; a program needn't handle non-finite values.
Results may differ from the reference program's by a relative error of at most 0.009.
Values may be sent and summed in bfloat16 or wider, within the bound.
No kernel may reach another device: no remote copies, remote signals or barrier semaphores. Data moves between devices by JAX's collectives and lax.ppermute only.
A program may use at most 128 MiB of HBM per device.

```python
import jax
import jax.numpy as jnp
from jax import lax

D = 5120
HEADS = 20
HEAD_DIM = 128
TOK_DEV = 512
TILE = 128
REACH = 3
TOKENS = 16384
N_SEQ = 32
N_HEAD = 4


def draw_queries(key, part):
    key = jax.random.fold_in(key, 1)
    base = 1.5 * jnp.clip(jax.random.normal(key, (TOKENS, HEADS, HEAD_DIM), jnp.float32), -6.0, 6.0)
    return base.astype(jnp.bfloat16)


def draw_key_rows(key, part):
    key = jax.random.fold_in(key, 2)
    base = 1.5 * jnp.clip(jax.random.normal(key, (TOKENS, HEADS, HEAD_DIM), jnp.float32), -6.0, 6.0)
    return base.astype(jnp.bfloat16)


def draw_tile_mask(key, part):
    key = jax.random.fold_in(key, 7)
    columns = TOK_DEV // TILE
    slab_size = 2 * columns
    slab_count = TOKENS // TILE // slab_size
    slab_keys = jax.random.split(key, slab_count)
    places = jax.vmap(lambda sub_key: jax.random.permutation(sub_key, slab_size))(slab_keys).reshape(-1).astype(jnp.int32)
    tile_ids = jnp.arange(TOKENS // TILE, dtype=jnp.int32)
    slab_of = tile_ids // slab_size
    row_of = places // columns
    column_of = places % columns
    near = jnp.abs(slab_of[:, None] - slab_of[None, :]) <= 1
    near = near & (jnp.abs(row_of[:, None] - row_of[None, :]) <= 1)
    near = near & (jnp.abs(column_of[:, None] - column_of[None, :]) <= 1)
    return near.astype(jnp.int32)


def block_levels(own_key, shape, pieces, least, high):
    level = 1.0
    for axis_at, shards_of in pieces:
        steps = jax.random.uniform(jax.random.fold_in(jax.random.fold_in(own_key, 6), axis_at), (shards_of,), jnp.float32, least / len(pieces), high / len(pieces))
        level = level * jnp.repeat(jnp.exp(steps), shape[axis_at] // shards_of).reshape((-1,) + (1,) * (len(shape) - 1 - axis_at))
    return level


def normal_values(key, dims, spread, bound, shards=(), kind=jnp.bfloat16):
    loudness = block_levels(key, dims, shards, -0.22, 0.18) if shards else 1.0
    result = jax.random.normal(key, dims, jnp.float32) * spread * loudness
    return jnp.minimum(jnp.maximum(result, -bound), bound).astype(kind)


def setup_inputs(seed: int = 0) -> dict:
    seeds = jax.random.split(jax.random.key(seed), 6)
    queries = draw_queries(jax.random.fold_in(seeds[5], 71), 0)
    key_rows = draw_key_rows(jax.random.fold_in(seeds[5], 71), 0)
    value_rows = normal_values(seeds[2], (TOKENS, HEADS, HEAD_DIM), 1.0, 6.0, ((0, 32), (1, 4)))
    out_weight = normal_values(seeds[3], (HEADS, HEAD_DIM, D), (HEADS * HEAD_DIM // 16) ** -0.5, 0.5, ((0, 4),))
    tile_mask = draw_tile_mask(jax.random.fold_in(seeds[5], 71), 0)
    return {"queries": queries, "key_rows": key_rows, "value_rows": value_rows, "out_weight": out_weight, "tile_mask": tile_mask}


def reference(queries, key_rows, value_rows, out_weight, tile_mask):
    tile_count = TOK_DEV // TILE
    offsets = jnp.arange(-REACH, REACH + 1, dtype=jnp.int32)

    def one_device(index):
        query_block = lax.dynamic_slice_in_dim(queries, (index * TOK_DEV).astype(jnp.int32), TOK_DEV, 0).astype(jnp.float32)
        holders = (index + offsets) % N_SEQ
        token_ids = (holders[:, None] * TOK_DEV + jnp.arange(TOK_DEV, dtype=jnp.int32)[None, :]).reshape(-1)
        key_sel = jnp.take(key_rows, token_ids, axis=0).astype(jnp.float32)
        value_sel = jnp.take(value_rows, token_ids, axis=0).astype(jnp.float32)
        tile_ids = (holders[:, None] * tile_count + jnp.arange(tile_count, dtype=jnp.int32)[None, :]).reshape(-1)
        mask_rows = lax.dynamic_slice_in_dim(tile_mask, (index * tile_count).astype(jnp.int32), tile_count, 0)
        tile_live = jnp.take(mask_rows, tile_ids, axis=1) > 0
        live_tokens = jnp.repeat(jnp.repeat(tile_live, TILE, axis=0), TILE, axis=1)
        scores = jnp.einsum("qhe,khe->hqk", query_block, key_sel) * (HEAD_DIM ** -0.5)
        masked = jnp.where(live_tokens[None], scores, -1.0e30)
        top = jnp.max(masked, axis=-1)
        weights = jnp.where(live_tokens[None], jnp.exp(scores - top[:, :, None]), 0.0)
        total = jnp.sum(weights, axis=-1)
        rounded = lax.optimization_barrier(weights.astype(jnp.bfloat16)).astype(jnp.float32)
        summed = jnp.einsum("hqk,khe->qhe", rounded, value_sel)
        return (summed / jnp.transpose(total)[:, :, None]).astype(jnp.bfloat16)

    attended = lax.map(one_device, jnp.arange(N_SEQ, dtype=jnp.int32)).reshape(TOKENS, HEADS, HEAD_DIM)
    heads_here = HEADS // N_HEAD
    mixed = jnp.zeros((TOKENS, D), jnp.float32)
    for group in range(N_HEAD):
        piece = attended[:, group * heads_here:(group + 1) * heads_here].reshape(TOKENS, heads_here * HEAD_DIM)
        weight_piece = out_weight[group * heads_here:(group + 1) * heads_here].reshape(heads_here * HEAD_DIM, D)
        partial_value = jnp.dot(piece, weight_piece, preferred_element_type=jnp.float32)
        mixed = mixed + partial_value
    return mixed.astype(jnp.bfloat16)
```

```python
import functools

import jax
import jax.numpy as jnp
from jax import lax
from jax.experimental import pallas as pl
from jax.experimental.pallas import tpu as pltpu
from jax.sharding import PartitionSpec as P

TILE = 128
SLAB = 8
ROW = 4
NEG = -1e30
LOG2E = 1.4426950408889634
AXES = ("seq", "head")
VMEM_LIMIT = 56 * 1024 * 1024


def route(rows, target):
    pairs = []
    for row in range(rows):
        for z in range(ROW):
            for yl in range(2):
                for c in range(2):
                    to = target(row, z, yl, c)
                    if to is not None:
                        dst = ((to[0] * ROW + to[1]) * 2 + to[2]) * 2 + to[3]
                        pairs.append((((row * ROW + z) * 2 + yl) * 2 + c, dst))
    return pairs


def send(block, rows, target):
    return lax.ppermute(block, AXES, route(rows, target))


def along_z(blocks, rows):
    plus, two, minus = (
        send(blocks[j - 1], rows, lambda r, z, yl, c, j=j: (r, (z + j) % ROW, yl, c)) for j in (1, 2, 3)
    )
    return [minus, two, plus]


def after(first, *then):
    tied = lax.optimization_barrier((tuple(first), tuple(then)))
    return list(tied[0]), list(tied[1])


def tile_places(tile_mask, row):
    padded = jnp.pad(tile_mask, SLAB)
    near = lax.dynamic_slice(padded, (row * 2 * SLAB, row * 2 * SLAB), (4 * SLAB, 4 * SLAB))
    live = (near > 0).astype(jnp.int32)
    grid = live.reshape(4, SLAB, 4, SLAB)
    within = jnp.stack([grid[t, :, t, :] for t in range(4)])
    degree = jnp.sum(within, axis=-1)
    ids = jnp.arange(SLAB, dtype=jnp.int32)
    edge = degree == 4
    first = jnp.min(jnp.where(edge[1], ids, SLAB))
    side_one = jnp.sum(jnp.where((ids == first)[:, None], live[SLAB : 2 * SLAB], 0), axis=0).reshape(4, SLAB)
    second = jnp.min(jnp.where(edge[2] & (side_one[2] > 0), ids, SLAB))
    side_two = jnp.sum(jnp.where((ids == second)[:, None], live[2 * SLAB : 3 * SLAB], 0), axis=0).reshape(4, SLAB)
    side = jnp.concatenate([side_one[:3], side_two[3:]]) > 0
    column = jnp.where(side, jnp.where(edge, 0, 1), jnp.where(edge, 3, 2))
    same = (column[:, :, None] == column[:, None, :]) & (ids[None, :] < ids[:, None])[None]
    place = column * 2 + jnp.sum(same.astype(jnp.int32), axis=-1)
    place = jnp.where(degree == 0, ids[None, :], place)
    return jnp.clip(place, 0, SLAB - 1).reshape(4 * SLAB)


ANYWHERE = pl.BlockSpec(memory_space=pltpu.VMEM)
SCALARS = pl.BlockSpec(memory_space=pltpu.SMEM)


def call(kernel, outs, scratch, operands, scalars, flops=0, moved=0, exps=0):
    return pl.pallas_call(
        kernel,
        out_shape=outs,
        in_specs=[SCALARS] * scalars + [ANYWHERE] * (len(operands) - scalars),
        out_specs=jax.tree.map(lambda _: ANYWHERE, outs),
        scratch_shapes=scratch,
        compiler_params=pltpu.CompilerParams(vmem_limit_bytes=VMEM_LIMIT),
        cost_estimate=pl.CostEstimate(flops=flops, bytes_accessed=moved, transcendentals=exps),
    )(*operands)


def pick_kernel(where_ref, own, one, two, three, up, down):
    z = where_ref[0]
    for at in range(ROW):

        @pl.when(z == at)
        def _():
            ring = (own, one, two, three)
            up[0] = ring[(2 - at) % ROW][...]
            up[1] = ring[(3 - at) % ROW][...]
            down[0] = ring[(0 - at) % ROW][...]
            down[1] = ring[(1 - at) % ROW][...]


def pick_one_kernel(where_ref, own, one, two, three, out):
    z = where_ref[0]
    for at in range(ROW):

        @pl.when(z == at)
        def _():
            ring = (own, one, two, three)
            base = 2 if at < 2 else 0
            out[0] = ring[(base - at) % ROW][...]
            out[1] = ring[(base + 1 - at) % ROW][...]


def spot(index):
    return pl.ds(pl.multiple_of(index * TILE, TILE), TILE)


def spread(where_ref, place_ref, ring, targets):
    z = where_ref[0]
    for j in range(ROW):
        block = lax.rem(z + j, ROW)
        for i in range(4):
            at = spot((block // 2) * SLAB + place_ref[SLAB + block * 4 + i])
            for target, piece in zip(targets, ring[j]):
                target[at, :] = piece[i * TILE : (i + 1) * TILE, :]


def softmax_rows(q, parts, valid, scale):
    scores = [
        lax.dot_general(q, keys, (((1,), (1,)), ((), ())), preferred_element_type=jnp.float32) for keys, _ in parts
    ]
    tops = [jnp.max(s, axis=-1, keepdims=True) for s in scores]
    tops[-1] = jnp.where(valid, tops[-1], NEG)
    top = functools.reduce(jnp.maximum, tops)
    total, summed = 0.0, 0.0
    for at, (s, (_, values)) in enumerate(zip(scores, parts)):
        weights = jnp.exp2((s - top) * (scale * LOG2E))
        part_total = jnp.sum(weights, axis=-1, keepdims=True)
        part_sum = jnp.dot(weights.astype(jnp.bfloat16), values, preferred_element_type=jnp.float32)
        if at == len(parts) - 1:
            part_total = jnp.where(valid, part_total, 0.0)
            part_sum = jnp.where(valid, part_sum, 0.0)
        total, summed = total + part_total, summed + part_sum
    return summed / total


WINDOW = ((0, 512), (0, 768), (256, 1024), (512, 1024))


def main_kernel(
    where_ref, place_ref, kv0, kv1, kv2, kv3, q0, q1, q2, q3, up, down, o0, o1, o2, o3, ks, vs, qs, os
):
    scale = q0.shape[-1] ** -0.5
    ring = [(kv.at[0], kv.at[1], q) for kv, q in zip((kv0, kv1, kv2, kv3), (q0, q1, q2, q3))]
    spread(where_ref, place_ref, ring, (ks.at[1024:3072], vs.at[1024:3072], qs))
    for side, first, slab in ((up, 0, 0), (down, 24, 3)):
        for b in range(2):
            for i in range(4):
                at = spot(slab * SLAB + place_ref[first + b * 4 + i])
                rows = slice(i * TILE, (i + 1) * TILE)
                ks[at, :] = side[b, 0, rows, :]
                vs[at, :] = side[b, 1, rows, :]
    for s in range(2):
        valid = where_ref[1 + s] > 0
        order = (1, 2, 0) if s == 0 else (1, 2, 3)
        for column, (low, high) in enumerate(WINDOW):
            rows = slice(s * 1024 + column * 256, s * 1024 + column * 256 + 256)
            parts = [(ks[t * 1024 + low : t * 1024 + high, :], vs[t * 1024 + low : t * 1024 + high, :]) for t in order]
            os[rows, :] = softmax_rows(qs[rows, :], parts, valid, scale).astype(jnp.bfloat16)
    z = where_ref[0]
    for j, out in enumerate((o0, o1, o2, o3)):
        block = lax.rem(z + j, ROW)
        for i in range(4):
            at = spot((block // 2) * SLAB + place_ref[SLAB + block * 4 + i])
            out[i * TILE : (i + 1) * TILE, :] = os[at, :]


def rest_kernel(where_ref, place_ref, kv0, kv1, kv2, kv3, q, halo, out, ks, vs):
    scale = q.shape[-1] ** -0.5
    z = where_ref[0]
    ring = [(kv.at[0], kv.at[1]) for kv in (kv0, kv1, kv2, kv3)]
    spread(where_ref, place_ref, ring, (ks.at[0:2048], vs.at[0:2048]))
    first = jnp.where(z < 2, 0, 24)
    valid = jnp.where(z < 2, where_ref[1], where_ref[2]) > 0
    for b in range(2):
        for i in range(4):
            at = spot(2 * SLAB + place_ref[first + b * 4 + i])
            rows = slice(i * TILE, (i + 1) * TILE)
            ks[at, :] = halo[b, 0, rows, :]
            vs[at, :] = halo[b, 1, rows, :]

    @pl.loop(0, 4)
    def _(i):
        column = place_ref[SLAB + z * 4 + i] // 2
        low = jnp.maximum(column - 1, 0) * 256
        here = spot(i)
        edge = (column == 0) | (column == 3)

        def work(width):
            parts = []
            for t in range(3):
                at = pl.ds(pl.multiple_of(t * 1024 + low, 256), width)
                parts.append((ks[at, :], vs[at, :]))
            out[here, :] = softmax_rows(q[here, :], parts, valid, scale).astype(jnp.bfloat16)

        @pl.when(edge)
        def _():
            work(512)

        @pl.when(jnp.logical_not(edge))
        def _():
            work(768)


def place_heads(z, main, rest, wide, base):
    for j in range(ROW):
        head = lax.rem(z + j, ROW)
        at = pl.multiple_of(base + head * TILE, TILE)
        wide[:, pl.ds(at, TILE)] = main[j]
    wide[:, base + ROW * TILE : base + (ROW + 1) * TILE] = rest[...]


def project_kernel(where_ref, m0, r0, w0, m1, r1, w1, out, wide):
    z = where_ref[0]
    place_heads(z, m0, r0, wide, 0)
    place_heads(z, m1, r1, wide, 640)

    @pl.loop(0, out.shape[1] // 256)
    def _(n):
        at = pl.ds(pl.multiple_of(n * 256, 256), 256)
        out[:, at] = jnp.dot(wide[:, :640], w0[:, at], preferred_element_type=jnp.float32) + jnp.dot(
            wide[:, 640:], w1[:, at], preferred_element_type=jnp.float32
        )


def finish_kernel(where_ref, m0, r0, w0, m1, r1, w1, before, out, wide):
    z = where_ref[0]
    place_heads(z, m0, r0, wide, 0)
    place_heads(z, m1, r1, wide, 640)

    @pl.loop(0, out.shape[1] // 256)
    def _(n):
        at = pl.ds(pl.multiple_of(n * 256, 256), 256)
        part = jnp.dot(wide[:, :640], w0[:, at], preferred_element_type=jnp.float32) + jnp.dot(
            wide[:, 640:], w1[:, at], preferred_element_type=jnp.float32
        )
        out[:, at] = (part + before[:, at]).astype(out.dtype)


def local(queries, key_rows, value_rows, out_weight, tile_mask):
    tok, heads, size = queries.shape
    rows = lax.axis_size("seq") // ROW
    seq, head = lax.axis_index("seq"), lax.axis_index("head")
    row, z = seq // ROW, seq % ROW
    yl, c = head // 2, head % 2
    bf = jnp.bfloat16
    wide_cols = out_weight.shape[-1] // 2
    cols = wide_cols // 2
    where = jnp.stack([z, (row > 0).astype(jnp.int32), (row < rows - 1).astype(jnp.int32), c]).astype(jnp.int32)

    with jax.named_scope("lay_out"):
        kv = jnp.stack([key_rows, value_rows]).transpose(2, 0, 1, 3)
        qh = queries.transpose(1, 0, 2)

    def ring_slices(array):
        return [lax.dynamic_index_in_dim(array, (z + j) % ROW, 0, keepdims=False) for j in range(ROW)]

    kv_own, *kv_out = ring_slices(kv)
    q_own, *q_out = ring_slices(qh)
    kv_rest, q_rest = kv[ROW], qh[ROW]

    with jax.named_scope("keys_values_z"):
        kv_in = along_z(kv_out, rows)
    with jax.named_scope("weights_y"):
        flat = out_weight.reshape(heads * size, 2 * wide_cols)
        theirs = lax.dynamic_slice_in_dim(flat, (1 - yl) * wide_cols, wide_cols, 1)

        def y_step(r, z, yl, c):
            yh, x = r // ROW, r % ROW
            y = (yh * 2 + yl + (1 if c == 0 else -1)) % 4
            return ((y // 2) * ROW + x, z, y % 2, c)

        w_far = send(theirs, rows, y_step)

    def sibling(block):
        return send(block, rows, lambda r, z, yl, c: (r, z, yl, 1 - c))

    with jax.named_scope("places"):
        place = tile_places(tile_mask, row)

    with jax.named_scope("queries_z"):
        kv_in, q_out = after(kv_in, *q_out)
        q_in = along_z(q_out, rows)
    with jax.named_scope("pick"):
        halo = jax.ShapeDtypeStruct((2, 2, tok, size), bf)
        to_next, to_prev = call(pick_kernel, (halo, halo), [], [where, kv_own, *kv_in], 1, moved=4 * 2**20)
    with jax.named_scope("keys_values_x"):
        from_prev = send(to_next, rows, lambda r, z, yl, c: (r + 1, z, yl, c) if r + 1 < rows else None)
        from_next = send(to_prev, rows, lambda r, z, yl, c: (r - 1, z, yl, c) if r > 0 else None)
    with jax.named_scope("rest_z"):
        q_in, (kv_rest_out,) = after(q_in, kv_rest)
        rest_in = along_z([kv_rest_out] * 3, rows)
    with jax.named_scope("main_attention"):
        block = jax.ShapeDtypeStruct((tok, size), bf)
        row_tok = ROW * tok
        o_own, *o_out = call(
            main_kernel,
            (block,) * 4,
            [
                pltpu.VMEM((2 * row_tok, size), bf),
                pltpu.VMEM((2 * row_tok, size), bf),
                pltpu.VMEM((row_tok, size), bf),
                pltpu.VMEM((row_tok, size), bf),
            ],
            [where, place, kv_own, *kv_in, q_own, *q_in, from_prev, from_next],
            2,
            flops=4 * 240 * TILE**3,
            moved=8 * 2**20,
            exps=240 * TILE**2,
        )
    with jax.named_scope("attended_z"):
        o_in = along_z(o_out, rows)
    with jax.named_scope("rest_pick"):
        to_rest = call(pick_one_kernel, halo, [], [where, kv_rest, *rest_in], 1, moved=2 * 2**20)
    with jax.named_scope("rest_x"):

        def rest_step(r, z, yl, c):
            to = r + 1 if z < 2 else r - 1
            return (to, z, yl, c) if 0 <= to < rows else None

        rest_halo = send(to_rest, rows, rest_step)
    with jax.named_scope("rest_attention"):
        o_rest = call(
            rest_kernel,
            block,
            [pltpu.VMEM((6 * tok, size), bf), pltpu.VMEM((6 * tok, size), bf)],
            [where, place, kv_rest, *rest_in, q_rest, rest_halo],
            2,
            flops=4 * 60 * TILE**3,
            moved=4 * 2**20,
            exps=60 * TILE**2,
        )

    def y_pair(block):
        return send(block, rows, lambda r, z, yl, c: (r, z, 1 - yl, c))

    main = jnp.stack([o_own, *o_in])
    with jax.named_scope("main_y"):
        main_far = y_pair(main)
    with jax.named_scope("main_core"):
        main_sib = sibling(main)
    with jax.named_scope("rest_y"):
        rest_far = y_pair(o_rest)
    with jax.named_scope("rest_core"):
        rest_sib = sibling(o_rest)
    with jax.named_scope("weights_core"):
        def halves(array, base):
            mine = lax.dynamic_slice_in_dim(array, base + c * cols, cols, 1)
            other = lax.dynamic_slice_in_dim(array, base + (1 - c) * cols, cols, 1)
            return mine, other

        w_own, w_own_other = halves(flat, yl * wide_cols)
        w_y, w_y_other = halves(w_far, 0)
        w_sib = sibling(w_own_other)
        w_y_sib = sibling(w_y_other)
    with jax.named_scope("main_far_core"):
        main_far_sib = sibling(main_far)
    with jax.named_scope("rest_far_core"):
        rest_far_sib = sibling(rest_far)
    wide = pltpu.VMEM((tok, 2 * heads * size), bf)
    with jax.named_scope("project"):
        near = call(
            project_kernel,
            jax.ShapeDtypeStruct((tok, cols), jnp.float32),
            [wide],
            [where, main, o_rest, w_own, main_sib, rest_sib, w_sib],
            1,
            flops=2 * tok * 2 * heads * size * cols,
            moved=8 * 2**20,
        )
    with jax.named_scope("finish"):
        return call(
            finish_kernel,
            jax.ShapeDtypeStruct((tok, cols), bf),
            [wide],
            [where, main_far, rest_far, w_y, main_far_sib, rest_far_sib, w_y_sib, near],
            1,
            flops=2 * tok * 2 * heads * size * cols,
            moved=8 * 2**20,
        )


def solution(mesh):
    placed = (
        P("seq", "head", None),
        P("seq", "head", None),
        P("seq", "head", None),
        P("head", None, None),
        P(),
    )
    return jax.shard_map(local, mesh=mesh, in_specs=placed, out_specs=P("seq", "head"), check_vma=False)
```

```python
import functools

import jax
import jax.numpy as jnp
from jax import lax
from jax.experimental import pallas as pl
from jax.experimental.pallas import tpu as pltpu
from jax.sharding import PartitionSpec as P

TILE = 128
SLAB = 8
ROW = 4
NEG = -1e30
LOG2E = 1.4426950408889634
AXES = ("seq", "head")
VMEM_LIMIT = 16 * 1024 * 1024


def route(rows, target):
    pairs = []
    for row in range(rows):
        for z in range(ROW):
            for yl in range(2):
                for c in range(2):
                    to = target(row, z, yl, c)
                    if to is not None:
                        dst = ((to[0] * ROW + to[1]) * 2 + to[2]) * 2 + to[3]
                        pairs.append((((row * ROW + z) * 2 + yl) * 2 + c, dst))
    return pairs


def send(block, rows, target):
    return lax.ppermute(block, AXES, route(rows, target))


def along_z(blocks, rows):
    plus, two, minus = (
        send(blocks[j - 1], rows, lambda r, z, yl, c, j=j: (r, (z + j) % ROW, yl, c)) for j in (1, 2, 3)
    )
    return [minus, two, plus]


def after(first, *then):
    return list(lax.optimization_barrier((tuple(first), tuple(then)))[1])


def places_kernel(where_ref, mask_ref, out):
    count = mask_ref.shape[0]
    start = where_ref[3]
    pick = lax.broadcasted_iota(jnp.int32, (4 * SLAB, count), 1) - lax.broadcasted_iota(jnp.int32, (4 * SLAB, count), 0)
    pick = jnp.where(pick == start, 1.0, 0.0)
    rows = jnp.dot(pick, (mask_ref[...] > 0).astype(jnp.float32), preferred_element_type=jnp.float32)
    near = lax.dot_general(rows, pick, (((1,), (1,)), ((), ())), preferred_element_type=jnp.float32)
    live = jnp.where(near > 0.5, 1, 0)
    shape = live.shape
    down = lax.broadcasted_iota(jnp.int32, shape, 0)
    across = lax.broadcasted_iota(jnp.int32, shape, 1)
    same_slab = (down // SLAB) == (across // SLAB)
    inside = jnp.where(same_slab, live, 0)
    lane = across[:1]
    degree = (jnp.sum(inside, axis=0, keepdims=True), jnp.sum(inside, axis=1, keepdims=True))
    edge_row = degree[0] == 4

    def beside(reference):
        return (
            jnp.sum(jnp.where(down == reference, live, 0), axis=0, keepdims=True),
            jnp.sum(jnp.where(across == reference, live, 0), axis=1, keepdims=True),
        )

    first = jnp.min(jnp.where(edge_row & (lane // SLAB == 1), lane, 4 * SLAB), axis=1, keepdims=True)
    one = beside(first)
    second = jnp.min(jnp.where(edge_row & (lane // SLAB == 2) & (one[0] > 0), lane, 4 * SLAB), axis=1, keepdims=True)
    two = beside(second)
    column = []
    for at, index in ((0, lane), (1, down[:, :1])):
        side = jnp.where(index < 3 * SLAB, one[at], two[at]) > 0
        middle = jnp.where(degree[at] == 4, 0, 1)
        column.append(jnp.where(side, middle, 3 - middle))
    twin = same_slab & (column[0] == column[1]) & (down < across)
    place = column[0] * 2 + jnp.sum(jnp.where(twin, 1, 0), axis=0, keepdims=True)
    place = jnp.where(degree[0] == 0, lane % SLAB, place)
    out[...] = jnp.clip(place, 0, SLAB - 1)


ANYWHERE = pl.BlockSpec(memory_space=pltpu.VMEM)
SCALARS = pl.BlockSpec(memory_space=pltpu.SMEM)


def call(kernel, outs, scratch, operands, scalars, flops=1024):
    return pl.pallas_call(
        kernel,
        out_shape=outs,
        in_specs=[SCALARS] * scalars + [ANYWHERE] * (len(operands) - scalars),
        out_specs=jax.tree.map(lambda _: ANYWHERE, outs),
        scratch_shapes=scratch,
        compiler_params=pltpu.CompilerParams(vmem_limit_bytes=VMEM_LIMIT),
        cost_estimate=pl.CostEstimate(flops=flops, bytes_accessed=1024, transcendentals=0),
    )(*operands)


def pick_kernel(where_ref, own, one, two, three, up, down):
    z = where_ref[0]
    for at in range(ROW):

        @pl.when(z == at)
        def _():
            ring = (own, one, two, three)
            for out, blocks in ((up, (2, 3)), (down, (0, 1))):
                for at_out, block in enumerate(blocks):
                    out[at_out] = ring[(block - at) % ROW][:2]


def pick_one_kernel(where_ref, own, one, two, three, out):
    z = where_ref[0]
    for at in range(ROW):

        @pl.when(z == at)
        def _():
            ring = (own, one, two, three)
            base = 2 if at < 2 else 0
            out[0] = ring[(base - at) % ROW][...]
            out[1] = ring[(base + 1 - at) % ROW][...]


def spot(index):
    return pl.ds(pl.multiple_of(index * TILE, TILE), TILE)


def spread(where_ref, place_ref, ring, targets):
    z = where_ref[0]
    for j in range(ROW):
        block = lax.rem(z + j, ROW)
        for i in range(4):
            at = spot((block // 2) * SLAB + place_ref[0, SLAB + block * 4 + i])
            for target, piece in zip(targets, ring[j]):
                target[at, :] = piece[i * TILE : (i + 1) * TILE, :]


def softmax_rows(q, parts, valid, scale):
    scores = [
        lax.dot_general(q, keys, (((1,), (1,)), ((), ())), preferred_element_type=jnp.float32) for keys, _ in parts
    ]
    tops = [jnp.max(s, axis=-1, keepdims=True) for s in scores]
    tops[-1] = jnp.where(valid, tops[-1], NEG)
    top = functools.reduce(jnp.maximum, tops)
    total, summed = 0.0, 0.0
    for at, (s, (_, values)) in enumerate(zip(scores, parts)):
        weights = jnp.exp2((s - top) * (scale * LOG2E))
        part_total = jnp.sum(weights, axis=-1, keepdims=True)
        part_sum = jnp.dot(weights.astype(jnp.bfloat16), values, preferred_element_type=jnp.float32)
        if at == len(parts) - 1:
            part_total = jnp.where(valid, part_total, 0.0)
            part_sum = jnp.where(valid, part_sum, 0.0)
        total, summed = total + part_total, summed + part_sum
    return summed / total


WINDOW = ((0, 512), (0, 768), (256, 1024), (512, 1024))


def piece_scores(q, keys):
    return lax.dot_general(q, keys, (((1,), (1,)), ((), ())), preferred_element_type=jnp.float32)


def near_kernel(where_ref, place_ref, kvq0, kvq1, kvq2, kvq3, qs, acc, stats, ks, vs):
    factor = ks.shape[-1] ** -0.5 * LOG2E
    ring = [(kvq.at[0], kvq.at[1], kvq.at[2]) for kvq in (kvq0, kvq1, kvq2, kvq3)]
    spread(where_ref, place_ref, ring, (ks, vs, qs))
    lane = lax.broadcasted_iota(jnp.int32, (256, 128), 1)
    for s in range(2):
        for column, (low, high) in enumerate(WINDOW):
            rows = slice(s * 1024 + column * 256, s * 1024 + column * 256 + 256)
            q = qs[rows, :]
            pieces = [slice(t * 1024 + low, t * 1024 + high) for t in range(2)]
            scores = [piece_scores(q, ks[piece, :]) for piece in pieces]
            top = functools.reduce(jnp.maximum, [jnp.max(p, axis=-1, keepdims=True) for p in scores])
            total, summed = 0.0, 0.0
            for piece, score in zip(pieces, scores):
                weights = jnp.exp2((score - top) * factor)
                total = total + jnp.sum(weights, axis=-1, keepdims=True)
                summed = summed + jnp.dot(
                    weights.astype(jnp.bfloat16), vs[piece, :], preferred_element_type=jnp.float32
                )
            acc[rows, :] = summed
            stats[rows, :] = jnp.where(lane == 0, top, total)


def halo_kernel(where_ref, place_ref, qs, acc, stats, up, down, o0, o1, o2, o3, ks, vs, os):
    factor = qs.shape[-1] ** -0.5 * LOG2E
    for side, first, slab in ((up, 0, 0), (down, 24, 1)):
        for b in range(2):
            for i in range(4):
                at = spot(slab * SLAB + place_ref[0, first + b * 4 + i])
                rows = slice(i * TILE, (i + 1) * TILE)
                ks[at, :] = side[b, 0, rows, :]
                vs[at, :] = side[b, 1, rows, :]
    for s in range(2):
        valid = where_ref[1 + s] > 0
        for column, (low, high) in enumerate(WINDOW):
            rows = slice(s * 1024 + column * 256, s * 1024 + column * 256 + 256)
            piece = slice(s * 1024 + low, s * 1024 + high)
            score = piece_scores(qs[rows, :], ks[piece, :])
            before = stats[rows, :]
            top_before, total_before = before[:, 0:1], before[:, 1:2]
            top = jnp.maximum(top_before, jnp.where(valid, jnp.max(score, axis=-1, keepdims=True), NEG))
            weights = jnp.exp2((score - top) * factor)
            total = jnp.where(valid, jnp.sum(weights, axis=-1, keepdims=True), 0.0)
            summed = jnp.dot(weights.astype(jnp.bfloat16), vs[piece, :], preferred_element_type=jnp.float32)
            summed = jnp.where(valid, summed, 0.0)
            shrink = jnp.exp2((top_before - top) * factor)
            total = total + total_before * shrink
            os[rows, :] = ((summed + acc[rows, :] * shrink) / total).astype(jnp.bfloat16)
    z = where_ref[0]
    for j, out in enumerate((o0, o1, o2, o3)):
        block = lax.rem(z + j, ROW)
        for i in range(4):
            at = spot((block // 2) * SLAB + place_ref[0, SLAB + block * 4 + i])
            out[i * TILE : (i + 1) * TILE, :] = os[at, :]


def rest_kernel(where_ref, place_ref, kv0, kv1, kv2, kv3, q, halo, out, ks, vs):
    scale = q.shape[-1] ** -0.5
    z = where_ref[0]
    ring = [(kv.at[0], kv.at[1]) for kv in (kv0, kv1, kv2, kv3)]
    spread(where_ref, place_ref, ring, (ks.at[0:2048], vs.at[0:2048]))
    first = jnp.where(z < 2, 0, 24)
    valid = jnp.where(z < 2, where_ref[1], where_ref[2]) > 0
    for b in range(2):
        for i in range(4):
            at = spot(2 * SLAB + place_ref[0, first + b * 4 + i])
            rows = slice(i * TILE, (i + 1) * TILE)
            ks[at, :] = halo[b, 0, rows, :]
            vs[at, :] = halo[b, 1, rows, :]

    @pl.loop(0, 4)
    def _(i):
        column = place_ref[0, SLAB + z * 4 + i] // 2
        low = jnp.maximum(column - 1, 0) * 256
        here = spot(i)
        edge = (column == 0) | (column == 3)

        def work(width):
            parts = []
            for t in range(3):
                at = pl.ds(pl.multiple_of(t * 1024 + low, 256), width)
                parts.append((ks[at, :], vs[at, :]))
            out[here, :] = softmax_rows(q[here, :], parts, valid, scale).astype(jnp.bfloat16)

        @pl.when(edge)
        def _():
            work(512)

        @pl.when(jnp.logical_not(edge))
        def _():
            work(768)


def place_heads(z, ring, wide, base):
    for j in range(ROW):
        head = lax.rem(z + j, ROW)
        at = pl.multiple_of(base + head * TILE, TILE)
        wide[:, pl.ds(at, TILE)] = ring[j]
    wide[:, base + ROW * TILE : base + (ROW + 1) * TILE] = ring[ROW]


def project_kernel(where_ref, m0, w0, m1, w1, out, wide):
    z = where_ref[0]
    place_heads(z, m0, wide, 0)
    place_heads(z, m1, wide, 640)

    @pl.loop(0, out.shape[1] // 256)
    def _(n):
        at = pl.ds(pl.multiple_of(n * 256, 256), 256)
        out[:, at] = jnp.dot(wide[:, :640], w0[:, at], preferred_element_type=jnp.float32) + jnp.dot(
            wide[:, 640:], w1[:, at], preferred_element_type=jnp.float32
        )


def finish_kernel(where_ref, m0, w0, m1, w1, before, out, wide):
    z = where_ref[0]
    place_heads(z, m0, wide, 0)
    place_heads(z, m1, wide, 640)

    @pl.loop(0, out.shape[1] // 256)
    def _(n):
        at = pl.ds(pl.multiple_of(n * 256, 256), 256)
        part = jnp.dot(wide[:, :640], w0[:, at], preferred_element_type=jnp.float32) + jnp.dot(
            wide[:, 640:], w1[:, at], preferred_element_type=jnp.float32
        )
        out[:, at] = (part + before[:, at]).astype(out.dtype)


def columns_kernel(where_ref, weight, out):
    out[...] = weight[0]


def local(queries, key_rows, value_rows, out_weight, tile_mask):
    tok, heads, size = queries.shape
    rows = lax.axis_size("seq") // ROW
    seq, head = lax.axis_index("seq"), lax.axis_index("head")
    row, z = seq // ROW, seq % ROW
    yl, c = head // 2, head % 2
    bf = jnp.bfloat16
    wide_cols = out_weight.shape[-1] // 2
    cols = wide_cols // 2
    row_tok = ROW * tok
    block = jax.ShapeDtypeStruct((tok, size), bf)
    halo = jax.ShapeDtypeStruct((2, 2, tok, size), bf)

    def ring_slices(array):
        return [lax.dynamic_index_in_dim(array, (z + j) % ROW, 0, keepdims=False) for j in range(ROW)]

    def sibling(piece):
        return send(piece, rows, lambda r, z, yl, c: (r, z, yl, 1 - c))

    def y_pair(piece):
        return send(piece, rows, lambda r, z, yl, c: (r, z, 1 - yl, c))

    with jax.named_scope("lay_out"):
        kvq = jnp.stack([key_rows, value_rows, queries]).transpose(2, 0, 1, 3)
        own, *out = [lax.dynamic_index_in_dim(kvq, (z + j) % ROW, 0, keepdims=False) for j in range(ROW)]
        kv_rest, q_rest = kvq[ROW, :2], kvq[ROW, 2]
    with jax.named_scope("head_z"):
        ring = along_z(out, rows)

    with jax.named_scope("weights_y"):
        lead = send(out[0][0, :16], rows, lambda r, z, yl, c: (r, (z + 1) % ROW, yl, c))
        (out_weight,) = after([lead], out_weight)
        where = jnp.stack([z, row > 0, row < rows - 1, row * 2 * SLAB - SLAB, yl]).astype(jnp.int32)
        theirs = pl.pallas_call(
            columns_kernel,
            out_shape=jax.ShapeDtypeStruct((heads * size, wide_cols), bf),
            grid_spec=pltpu.PrefetchScalarGridSpec(
                num_scalar_prefetch=1,
                grid=(heads,),
                in_specs=[pl.BlockSpec((1, size, wide_cols), lambda h, where: (h, 0, 1 - where[4]))],
                out_specs=pl.BlockSpec((size, wide_cols), lambda h, where: (h, 0)),
            ),
            compiler_params=pltpu.CompilerParams(vmem_limit_bytes=VMEM_LIMIT),
            cost_estimate=pl.CostEstimate(flops=2 * 10**10, bytes_accessed=1024, transcendentals=0),
        )(where, out_weight)

        def y_step(r, z, yl, c):
            yh, x = r // ROW, r % ROW
            y = (yh * 2 + yl + (1 if c == 0 else -1)) % 4
            return ((y // 2) * ROW + x, z, y % 2, c)

        w_far = send(theirs, rows, y_step)

    with jax.named_scope("pick"):
        to_next, to_prev = call(pick_kernel, (halo, halo), [], [where, own, *ring], 1)
    with jax.named_scope("head_x"):
        from_prev = send(to_next, rows, lambda r, z, yl, c: (r + 1, z, yl, c) if r + 1 < rows else None)
        from_next = send(to_prev, rows, lambda r, z, yl, c: (r - 1, z, yl, c) if r > 0 else None)
    with jax.named_scope("places"):
        (tile_mask,) = after([to_next], tile_mask)
        place = call(
            places_kernel, jax.ShapeDtypeStruct((1, 4 * SLAB), jnp.int32), [], [where, tile_mask], 1, flops=10**10
        )
    with jax.named_scope("rest_z"):
        (kv_rest,) = after([place], kv_rest)
        rest_in = along_z([kv_rest] * 3, rows)
    with jax.named_scope("near_attention"):
        qs, acc, stats = call(
            near_kernel,
            (
                jax.ShapeDtypeStruct((row_tok, size), bf),
                jax.ShapeDtypeStruct((row_tok, size), jnp.float32),
                jax.ShapeDtypeStruct((row_tok, size), jnp.float32),
            ),
            [pltpu.VMEM((row_tok, size), bf), pltpu.VMEM((row_tok, size), bf)],
            [where, place, own, *ring],
            2,
            flops=10**10,
        )
    with jax.named_scope("rest_pick"):
        to_rest = call(pick_one_kernel, halo, [], [where, kv_rest, *rest_in], 1)
    with jax.named_scope("rest_x"):

        def rest_step(r, z, yl, c):
            to = r + 1 if z < 2 else r - 1
            return (to, z, yl, c) if 0 <= to < rows else None

        rest_halo = send(to_rest, rows, rest_step)
    with jax.named_scope("halo_attention"):
        (from_prev,) = after([to_rest], from_prev)
        o_own, *o_out = call(
            halo_kernel,
            (block,) * 4,
            [pltpu.VMEM((row_tok, size), bf)] * 3,
            [where, place, qs, acc, stats, from_prev, from_next],
            2,
            flops=10**10,
        )
    with jax.named_scope("attended_z"):
        o_in = along_z(o_out, rows)
    with jax.named_scope("rest_attention"):
        (rest_halo,) = after([o_own], rest_halo)
        o_rest = call(
            rest_kernel,
            block,
            [pltpu.VMEM((6 * tok, size), bf), pltpu.VMEM((6 * tok, size), bf)],
            [where, place, kv_rest, *rest_in, q_rest, rest_halo],
            2,
            flops=10**10,
        )
    mine = jnp.stack([o_own, *o_in, o_rest])
    with jax.named_scope("attended_y"):
        far = y_pair(mine)
    with jax.named_scope("attended_core"):
        mine_sib = sibling(mine)
    with jax.named_scope("weights_core"):

        def halves(array, base):
            mine = lax.dynamic_slice_in_dim(array, base + c * cols, cols, 1)
            other = lax.dynamic_slice_in_dim(array, base + (1 - c) * cols, cols, 1)
            return mine, other

        flat, w_far = after([mine], out_weight.reshape(heads * size, 2 * wide_cols), w_far)
        w_own, w_own_other = halves(flat, yl * wide_cols)
        w_y, w_y_other = halves(w_far, 0)
        w_sib = sibling(jnp.stack([w_own_other, w_y_other]))
    wide = pltpu.VMEM((tok, 2 * heads * size), bf)
    with jax.named_scope("project"):
        near = call(
            project_kernel,
            jax.ShapeDtypeStruct((tok, cols), jnp.float32),
            [wide],
            [where, mine, w_own, mine_sib, w_sib[0]],
            1,
            flops=10**10,
        )
    with jax.named_scope("far_core"):
        (far,) = after([near], far)
        far_sib = sibling(far)
    with jax.named_scope("finish"):
        return call(
            finish_kernel,
            jax.ShapeDtypeStruct((tok, cols), bf),
            [wide],
            [where, far, w_y, far_sib, w_sib[1], near],
            1,
        )


def solution(mesh):
    placed = (
        P("seq", "head", None),
        P("seq", "head", None),
        P("seq", "head", None),
        P("head", None, None),
        P(),
    )
    return jax.shard_map(local, mesh=mesh, in_specs=placed, out_specs=P("seq", "head"), check_vma=False)
```

```python
import functools

import jax
import jax.numpy as jnp
from jax import lax
from jax.experimental import pallas as pl
from jax.experimental.pallas import tpu as pltpu
from jax.sharding import PartitionSpec as P

TILE = 128
SLAB = 8
ROW = 4
NEG = -1e30
LOG2E = 1.4426950408889634
AXES = ("seq", "head")
VMEM_LIMIT = 16 * 1024 * 1024


def route(rows, target):
    pairs = []
    for row in range(rows):
        for z in range(ROW):
            for yl in range(2):
                for c in range(2):
                    to = target(row, z, yl, c)
                    if to is not None:
                        dst = ((to[0] * ROW + to[1]) * 2 + to[2]) * 2 + to[3]
                        pairs.append((((row * ROW + z) * 2 + yl) * 2 + c, dst))
    return pairs


def send(block, rows, target):
    return lax.ppermute(block, AXES, route(rows, target))


def along_z(blocks, rows):
    plus, two, minus = (
        send(blocks[j - 1], rows, lambda r, z, yl, c, j=j: (r, (z + j) % ROW, yl, c)) for j in (1, 2, 3)
    )
    return [minus, two, plus]


def together(*arrays):
    return lax.optimization_barrier(arrays)


def places_kernel(where_ref, mask_ref, rest_ref, out, rest_out):
    rest_out[...] = rest_ref[...]
    count = mask_ref.shape[0]
    start = where_ref[3]
    pick = lax.broadcasted_iota(jnp.int32, (4 * SLAB, count), 1) - lax.broadcasted_iota(jnp.int32, (4 * SLAB, count), 0)
    pick = jnp.where(pick == start, 1.0, 0.0)
    rows = jnp.dot(pick, (mask_ref[...] > 0).astype(jnp.float32), preferred_element_type=jnp.float32)
    near = lax.dot_general(rows, pick, (((1,), (1,)), ((), ())), preferred_element_type=jnp.float32)
    live = jnp.where(near > 0.5, 1, 0)
    shape = live.shape
    down = lax.broadcasted_iota(jnp.int32, shape, 0)
    across = lax.broadcasted_iota(jnp.int32, shape, 1)
    same_slab = (down // SLAB) == (across // SLAB)
    inside = jnp.where(same_slab, live, 0)
    lane = across[:1]
    degree = (jnp.sum(inside, axis=0, keepdims=True), jnp.sum(inside, axis=1, keepdims=True))
    edge_row = degree[0] == 4

    def beside(reference):
        return (
            jnp.sum(jnp.where(down == reference, live, 0), axis=0, keepdims=True),
            jnp.sum(jnp.where(across == reference, live, 0), axis=1, keepdims=True),
        )

    first = jnp.min(jnp.where(edge_row & (lane // SLAB == 1), lane, 4 * SLAB), axis=1, keepdims=True)
    one = beside(first)
    second = jnp.min(jnp.where(edge_row & (lane // SLAB == 2) & (one[0] > 0), lane, 4 * SLAB), axis=1, keepdims=True)
    two = beside(second)
    column = []
    for at, index in ((0, lane), (1, down[:, :1])):
        side = jnp.where(index < 3 * SLAB, one[at], two[at]) > 0
        middle = jnp.where(degree[at] == 4, 0, 1)
        column.append(jnp.where(side, middle, 3 - middle))
    twin = same_slab & (column[0] == column[1]) & (down < across)
    place = column[0] * 2 + jnp.sum(jnp.where(twin, 1, 0), axis=0, keepdims=True)
    place = jnp.where(degree[0] == 0, lane % SLAB, place)
    out[...] = jnp.clip(place, 0, SLAB - 1)


ANYWHERE = pl.BlockSpec(memory_space=pltpu.VMEM)
SCALARS = pl.BlockSpec(memory_space=pltpu.SMEM)


def call(kernel, outs, scratch, operands, scalars, flops=1024, later=(), far=0):
    held = len(operands) - scalars - far

    def body(*refs):
        at = len(operands)
        kernel(*refs[:at], *refs[at + len(later) :])

    return pl.pallas_call(
        body,
        out_shape=outs,
        in_specs=[SCALARS] * scalars + [ANYWHERE] * held + [pl.BlockSpec(memory_space=pl.ANY)] * (far + len(later)),
        out_specs=jax.tree.map(lambda _: ANYWHERE, outs),
        scratch_shapes=scratch,
        compiler_params=pltpu.CompilerParams(vmem_limit_bytes=VMEM_LIMIT),
        cost_estimate=pl.CostEstimate(flops=flops, bytes_accessed=1024, transcendentals=0),
    )(*operands, *later)


def pick_kernel(where_ref, own, one, two, three, up, down):
    z = where_ref[0]
    for at in range(ROW):

        @pl.when(z == at)
        def _():
            ring = (own, one, two, three)
            for out, blocks in ((up, (2, 3)), (down, (0, 1))):
                for at_out, block in enumerate(blocks):
                    out[at_out] = ring[(block - at) % ROW][:2]


def pick_one_kernel(where_ref, own, one, two, three, out):
    z = where_ref[0]
    for at in range(ROW):

        @pl.when(z == at)
        def _():
            ring = (own, one, two, three)
            base = 2 if at < 2 else 0
            out[0] = ring[(base - at) % ROW][...]
            out[1] = ring[(base + 1 - at) % ROW][...]


def spot(index):
    return pl.ds(pl.multiple_of(index * TILE, TILE), TILE)


def spread(where_ref, place_ref, ring, targets):
    z = where_ref[0]
    for j in range(ROW):
        block = lax.rem(z + j, ROW)
        for i in range(4):
            at = spot((block // 2) * SLAB + place_ref[0, SLAB + block * 4 + i])
            for target, piece in zip(targets, ring[j]):
                target[at, :] = piece[i * TILE : (i + 1) * TILE, :]


def softmax_rows(q, parts, valid, scale):
    scores = [
        lax.dot_general(q, keys, (((1,), (1,)), ((), ())), preferred_element_type=jnp.float32) for keys, _ in parts
    ]
    tops = [jnp.max(s, axis=-1, keepdims=True) for s in scores]
    tops[-1] = jnp.where(valid, tops[-1], NEG)
    top = functools.reduce(jnp.maximum, tops)
    total, summed = 0.0, 0.0
    for at, (s, (_, values)) in enumerate(zip(scores, parts)):
        weights = jnp.exp2((s - top) * (scale * LOG2E))
        part_total = jnp.sum(weights, axis=-1, keepdims=True)
        part_sum = jnp.dot(weights.astype(jnp.bfloat16), values, preferred_element_type=jnp.float32)
        if at == len(parts) - 1:
            part_total = jnp.where(valid, part_total, 0.0)
            part_sum = jnp.where(valid, part_sum, 0.0)
        total, summed = total + part_total, summed + part_sum
    return summed / total


WINDOW = ((0, 512), (0, 768), (256, 1024), (512, 1024))


def piece_scores(q, keys):
    return lax.dot_general(q, keys, (((1,), (1,)), ((), ())), preferred_element_type=jnp.float32)


def near_kernel(where_ref, place_ref, kvq0, kvq1, kvq2, kvq3, qs, acc, stats, ks, vs):
    factor = ks.shape[-1] ** -0.5 * LOG2E
    ring = [(kvq.at[0], kvq.at[1], kvq.at[2]) for kvq in (kvq0, kvq1, kvq2, kvq3)]
    spread(where_ref, place_ref, ring, (ks, vs, qs))
    lane = lax.broadcasted_iota(jnp.int32, (256, 128), 1)
    for s in range(2):
        for column, (low, high) in enumerate(WINDOW):
            rows = slice(s * 1024 + column * 256, s * 1024 + column * 256 + 256)
            q = qs[rows, :]
            pieces = [slice(t * 1024 + low, t * 1024 + high) for t in range(2)]
            scores = [piece_scores(q, ks[piece, :]) for piece in pieces]
            top = functools.reduce(jnp.maximum, [jnp.max(p, axis=-1, keepdims=True) for p in scores])
            total, summed = 0.0, 0.0
            for piece, score in zip(pieces, scores):
                weights = jnp.exp2((score - top) * factor)
                total = total + jnp.sum(weights, axis=-1, keepdims=True)
                summed = summed + jnp.dot(
                    weights.astype(jnp.bfloat16), vs[piece, :], preferred_element_type=jnp.float32
                )
            acc[rows, :] = summed
            stats[rows, :] = jnp.where(lane == 0, top, total)


def halo_kernel(where_ref, place_ref, qs, acc, stats, up, down, o0, o1, o2, o3, ks, vs, os):
    factor = qs.shape[-1] ** -0.5 * LOG2E
    for side, first, slab in ((up, 0, 0), (down, 24, 1)):
        for b in range(2):
            for i in range(4):
                at = spot(slab * SLAB + place_ref[0, first + b * 4 + i])
                rows = slice(i * TILE, (i + 1) * TILE)
                ks[at, :] = side[b, 0, rows, :]
                vs[at, :] = side[b, 1, rows, :]
    for s in range(2):
        valid = where_ref[1 + s] > 0
        for column, (low, high) in enumerate(WINDOW):
            rows = slice(s * 1024 + column * 256, s * 1024 + column * 256 + 256)
            piece = slice(s * 1024 + low, s * 1024 + high)
            score = piece_scores(qs[rows, :], ks[piece, :])
            before = stats[rows, :]
            top_before, total_before = before[:, 0:1], before[:, 1:2]
            top = jnp.maximum(top_before, jnp.where(valid, jnp.max(score, axis=-1, keepdims=True), NEG))
            weights = jnp.exp2((score - top) * factor)
            total = jnp.where(valid, jnp.sum(weights, axis=-1, keepdims=True), 0.0)
            summed = jnp.dot(weights.astype(jnp.bfloat16), vs[piece, :], preferred_element_type=jnp.float32)
            summed = jnp.where(valid, summed, 0.0)
            shrink = jnp.exp2((top_before - top) * factor)
            total = total + total_before * shrink
            os[rows, :] = ((summed + acc[rows, :] * shrink) / total).astype(jnp.bfloat16)
    z = where_ref[0]
    for j, out in enumerate((o0, o1, o2, o3)):
        block = lax.rem(z + j, ROW)
        for i in range(4):
            at = spot((block // 2) * SLAB + place_ref[0, SLAB + block * 4 + i])
            out[i * TILE : (i + 1) * TILE, :] = os[at, :]


def rest_kernel(where_ref, place_ref, kv0, kv1, kv2, kv3, q, halo, out, ks, vs):
    scale = q.shape[-1] ** -0.5
    z = where_ref[0]
    ring = [(kv.at[0], kv.at[1]) for kv in (kv0, kv1, kv2, kv3)]
    spread(where_ref, place_ref, ring, (ks.at[0:2048], vs.at[0:2048]))
    first = jnp.where(z < 2, 0, 24)
    valid = jnp.where(z < 2, where_ref[1], where_ref[2]) > 0
    for b in range(2):
        for i in range(4):
            at = spot(2 * SLAB + place_ref[0, first + b * 4 + i])
            rows = slice(i * TILE, (i + 1) * TILE)
            ks[at, :] = halo[b, 0, rows, :]
            vs[at, :] = halo[b, 1, rows, :]

    @pl.loop(0, 4)
    def _(i):
        column = place_ref[0, SLAB + z * 4 + i] // 2
        low = jnp.maximum(column - 1, 0) * 256
        here = spot(i)
        edge = (column == 0) | (column == 3)

        def work(width):
            parts = []
            for t in range(3):
                at = pl.ds(pl.multiple_of(t * 1024 + low, 256), width)
                parts.append((ks[at, :], vs[at, :]))
            out[here, :] = softmax_rows(q[here, :], parts, valid, scale).astype(jnp.bfloat16)

        @pl.when(edge)
        def _():
            work(512)

        @pl.when(jnp.logical_not(edge))
        def _():
            work(768)


def place_heads(z, ring, wide, base):
    for j in range(ROW):
        head = lax.rem(z + j, ROW)
        at = pl.multiple_of(base + head * TILE, TILE)
        wide[:, pl.ds(at, TILE)] = ring[j]
    wide[:, base + ROW * TILE : base + (ROW + 1) * TILE] = ring[ROW]


def project_kernel(where_ref, m0, w0, m1, w1, out, wide):
    z = where_ref[0]
    place_heads(z, m0, wide, 0)
    place_heads(z, m1, wide, 640)

    @pl.loop(0, out.shape[1] // 256)
    def _(n):
        at = pl.ds(pl.multiple_of(n * 256, 256), 256)
        out[:, at] = jnp.dot(wide[:, :640], w0[:, at], preferred_element_type=jnp.float32) + jnp.dot(
            wide[:, 640:], w1[:, at], preferred_element_type=jnp.float32
        )


def finish_kernel(where_ref, m0, w0, m1, w1, before, out, wide):
    z = where_ref[0]
    place_heads(z, m0, wide, 0)
    place_heads(z, m1, wide, 640)

    @pl.loop(0, out.shape[1] // 256)
    def _(n):
        at = pl.ds(pl.multiple_of(n * 256, 256), 256)
        part = jnp.dot(wide[:, :640], w0[:, at], preferred_element_type=jnp.float32) + jnp.dot(
            wide[:, 640:], w1[:, at], preferred_element_type=jnp.float32
        )
        out[:, at] = (part + before[:, at]).astype(out.dtype)


def fetch(copies):
    for copy in copies:
        copy.start()
    for copy in copies:
        copy.wait()


def theirs_kernel(where_ref, weight, out, sem):
    heads, _, width = weight.shape
    at = pl.ds(pl.multiple_of((1 - where_ref[4]) * (width // 2), TILE), width // 2)
    fetch([pltpu.make_async_copy(weight.at[h, :, at], out.at[spot(h), :], sem.at[h]) for h in range(heads)])


def own_halves_kernel(where_ref, weight, mine, other, sem):
    heads, _, width = weight.shape
    cols, c = width // 4, where_ref[5]
    copies = []
    for k, (out, core) in enumerate(((mine, c), (other, 1 - c))):
        at = pl.ds(pl.multiple_of((where_ref[4] * 2 + core) * cols, TILE), cols)
        copies += [
            pltpu.make_async_copy(weight.at[h, :, at], out.at[spot(h), :], sem.at[k * heads + h]) for h in range(heads)
        ]
    fetch(copies)


def far_halves_kernel(where_ref, weight, mine, other, sem):
    cols, c = weight.shape[1] // 2, where_ref[5]
    copies = []
    for k, (out, core) in enumerate(((mine, c), (other, 1 - c))):
        at = pl.ds(pl.multiple_of(core * cols, TILE), cols)
        copies.append(pltpu.make_async_copy(weight.at[:, at], out, sem.at[k]))
    fetch(copies)


def local(queries, key_rows, value_rows, out_weight, tile_mask):
    tok, heads, size = queries.shape
    rows = lax.axis_size("seq") // ROW
    seq, head = lax.axis_index("seq"), lax.axis_index("head")
    row, z = seq // ROW, seq % ROW
    yl, c = head // 2, head % 2
    bf = jnp.bfloat16
    wide_cols = out_weight.shape[-1] // 2
    cols = wide_cols // 2
    row_tok = ROW * tok
    block = jax.ShapeDtypeStruct((tok, size), bf)
    halo = jax.ShapeDtypeStruct((2, 2, tok, size), bf)

    def ring_slices(array):
        return [lax.dynamic_index_in_dim(array, (z + j) % ROW, 0, keepdims=False) for j in range(ROW)]

    def sibling(piece):
        return send(piece, rows, lambda r, z, yl, c: (r, z, yl, 1 - c))

    def y_pair(piece):
        return send(piece, rows, lambda r, z, yl, c: (r, z, 1 - yl, c))

    with jax.named_scope("lay_out"):
        kvq = jnp.stack([key_rows, value_rows, queries]).transpose(2, 0, 1, 3)
        own, *out = [lax.dynamic_index_in_dim(kvq, (z + j) % ROW, 0, keepdims=False) for j in range(ROW)]
        kv_rest, q_rest = kvq[ROW, :2], kvq[ROW, 2]
    with jax.named_scope("head_z"):
        ring = along_z(out, rows)

    with jax.named_scope("weights_y"):
        where = jnp.stack([z, row > 0, row < rows - 1, row * 2 * SLAB - SLAB, yl, c]).astype(jnp.int32)
        theirs = call(
            theirs_kernel,
            jax.ShapeDtypeStruct((heads * size, wide_cols), bf),
            [pltpu.SemaphoreType.DMA((heads,))],
            [where, out_weight],
            1,
            later=out[:1],
            far=1,
            flops=8000000000,
        )

        def y_step(r, z, yl, c):
            yh, x = r // ROW, r % ROW
            y = (yh * 2 + yl + (1 if c == 0 else -1)) % 4
            return ((y // 2) * ROW + x, z, y % 2, c)

        w_far = send(theirs, rows, y_step)

    with jax.named_scope("pick"):
        to_next, to_prev = call(pick_kernel, (halo, halo), [], [where, own, *ring], 1)
    with jax.named_scope("head_x"):
        from_prev = send(to_next, rows, lambda r, z, yl, c: (r + 1, z, yl, c) if r + 1 < rows else None)
        from_next = send(to_prev, rows, lambda r, z, yl, c: (r - 1, z, yl, c) if r > 0 else None)
    with jax.named_scope("places"):
        place, kv_rest = call(
            places_kernel,
            (jax.ShapeDtypeStruct((1, 4 * SLAB), jnp.int32), jax.ShapeDtypeStruct((2, tok, size), bf)),
            [],
            [where, tile_mask, kv_rest],
            1,
            later=[to_next],
            flops=8000000000,
        )
    with jax.named_scope("rest_z"):
        rest_in = along_z([kv_rest] * 3, rows)
    with jax.named_scope("rest_pick"):
        to_rest = call(pick_one_kernel, halo, [], [where, kv_rest, *rest_in], 1)
    with jax.named_scope("rest_x"):

        def rest_step(r, z, yl, c):
            to = r + 1 if z < 2 else r - 1
            return (to, z, yl, c) if 0 <= to < rows else None

        rest_halo = send(to_rest, rows, rest_step)
    with jax.named_scope("near_attention"):
        qs, acc, stats = call(
            near_kernel,
            (
                jax.ShapeDtypeStruct((row_tok, size), bf),
                jax.ShapeDtypeStruct((row_tok, size), jnp.float32),
                jax.ShapeDtypeStruct((row_tok, size), jnp.float32),
            ),
            [pltpu.VMEM((row_tok, size), bf), pltpu.VMEM((row_tok, size), bf)],
            [where, place, own, *ring],
            2,
            flops=8000000000,
        )
    with jax.named_scope("halo_attention"):
        o_own, *o_out = call(
            halo_kernel,
            (block,) * 4,
            [pltpu.VMEM((row_tok, size), bf)] * 3,
            [where, place, qs, acc, stats, from_prev, from_next],
            2,
            later=[to_rest],
            flops=1000000000,
        )
    with jax.named_scope("attended_z"):
        o_in = along_z(o_out, rows)
    half = jax.ShapeDtypeStruct((heads * size, cols), bf)
    with jax.named_scope("weights_core"):
        w_own, w_own_other = call(
            own_halves_kernel,
            (half, half),
            [pltpu.SemaphoreType.DMA((2 * heads,))],
            [where, out_weight],
            1,
            later=[o_own],
            far=1,
        )
        w_sib = sibling(w_own_other)
    with jax.named_scope("rest_attention"):
        o_rest = call(
            rest_kernel,
            block,
            [pltpu.VMEM((6 * tok, size), bf), pltpu.VMEM((6 * tok, size), bf)],
            [where, place, kv_rest, *rest_in, q_rest, rest_halo],
            2,
            later=[o_own],
            flops=3000000000,
        )
    with jax.named_scope("weights_far_core"):
        w_y, w_y_other = call(
            far_halves_kernel,
            (half, half),
            [pltpu.SemaphoreType.DMA((2,))],
            [where, w_far],
            1,
            later=[o_rest],
            far=1,
            flops=1000000000,
        )
        w_y_sib = sibling(w_y_other)
    mine = jnp.stack([o_own, *o_in, o_rest])
    with jax.named_scope("attended_y"):
        far = y_pair(mine)
    with jax.named_scope("attended_core"):
        mine_sib = sibling(mine)
    wide = pltpu.VMEM((tok, 2 * heads * size), bf)
    with jax.named_scope("project"):
        near = call(
            project_kernel,
            jax.ShapeDtypeStruct((tok, cols), jnp.float32),
            [wide],
            [where, mine, w_own, mine_sib, w_sib],
            1,
            flops=10000000000,
        )
    with jax.named_scope("far_core"):
        near, far = together(near, far)
        far_sib = sibling(far)
    with jax.named_scope("finish"):
        return call(
            finish_kernel,
            jax.ShapeDtypeStruct((tok, cols), bf),
            [wide],
            [where, far, w_y, far_sib, w_y_sib, near],
            1,
        )


def solution(mesh):
    placed = (
        P("seq", "head", None),
        P("seq", "head", None),
        P("seq", "head", None),
        P("head", None, None),
        P(),
    )
    return jax.shard_map(local, mesh=mesh, in_specs=placed, out_specs=P("seq", "head"), check_vma=False)
```

```python
import functools

import jax
import jax.numpy as jnp
from jax import lax
from jax.experimental import pallas as pl
from jax.experimental.pallas import tpu as pltpu
from jax.sharding import PartitionSpec as P

TILE = 128
SLAB = 8
ROW = 4
NEG = -1e30
LOG2E = 1.4426950408889634
AXES = ("seq", "head")
VMEM_LIMIT = 16 * 1024 * 1024


def route(rows, target):
    pairs = []
    for row in range(rows):
        for z in range(ROW):
            for yl in range(2):
                for c in range(2):
                    to = target(row, z, yl, c)
                    if to is not None:
                        dst = ((to[0] * ROW + to[1]) * 2 + to[2]) * 2 + to[3]
                        pairs.append((((row * ROW + z) * 2 + yl) * 2 + c, dst))
    return pairs


def send(block, rows, target):
    return lax.ppermute(block, AXES, route(rows, target))


def along_z(blocks, rows):
    plus, two, minus = (
        send(blocks[j - 1], rows, lambda r, z, yl, c, j=j: (r, (z + j) % ROW, yl, c)) for j in (1, 2, 3)
    )
    return [minus, two, plus]


def together(*arrays):
    return lax.optimization_barrier(arrays)


def places_kernel(where_ref, mask_ref, rest_ref, out, rest_out):
    rest_out[...] = rest_ref[...]
    count = mask_ref.shape[0]
    start = where_ref[3]
    pick = lax.broadcasted_iota(jnp.int32, (4 * SLAB, count), 1) - lax.broadcasted_iota(jnp.int32, (4 * SLAB, count), 0)
    pick = jnp.where(pick == start, 1.0, 0.0)
    rows = jnp.dot(pick, (mask_ref[...] > 0).astype(jnp.float32), preferred_element_type=jnp.float32)
    near = lax.dot_general(rows, pick, (((1,), (1,)), ((), ())), preferred_element_type=jnp.float32)
    live = jnp.where(near > 0.5, 1, 0)
    shape = live.shape
    down = lax.broadcasted_iota(jnp.int32, shape, 0)
    across = lax.broadcasted_iota(jnp.int32, shape, 1)
    same_slab = (down // SLAB) == (across // SLAB)
    inside = jnp.where(same_slab, live, 0)
    lane = across[:1]
    degree = (jnp.sum(inside, axis=0, keepdims=True), jnp.sum(inside, axis=1, keepdims=True))
    edge_row = degree[0] == 4

    def beside(reference):
        return (
            jnp.sum(jnp.where(down == reference, live, 0), axis=0, keepdims=True),
            jnp.sum(jnp.where(across == reference, live, 0), axis=1, keepdims=True),
        )

    first = jnp.min(jnp.where(edge_row & (lane // SLAB == 1), lane, 4 * SLAB), axis=1, keepdims=True)
    one = beside(first)
    second = jnp.min(jnp.where(edge_row & (lane // SLAB == 2) & (one[0] > 0), lane, 4 * SLAB), axis=1, keepdims=True)
    two = beside(second)
    column = []
    for at, index in ((0, lane), (1, down[:, :1])):
        side = jnp.where(index < 3 * SLAB, one[at], two[at]) > 0
        middle = jnp.where(degree[at] == 4, 0, 1)
        column.append(jnp.where(side, middle, 3 - middle))
    twin = same_slab & (column[0] == column[1]) & (down < across)
    place = column[0] * 2 + jnp.sum(jnp.where(twin, 1, 0), axis=0, keepdims=True)
    place = jnp.where(degree[0] == 0, lane % SLAB, place)
    out[...] = jnp.clip(place, 0, SLAB - 1)


ANYWHERE = pl.BlockSpec(memory_space=pltpu.VMEM)
SCALARS = pl.BlockSpec(memory_space=pltpu.SMEM)


def call(kernel, outs, scratch, operands, scalars, flops=1024, later=(), far=0, out_spec=ANYWHERE):
    held = len(operands) - scalars - far

    def body(*refs):
        at = len(operands)
        kernel(*refs[:at], *refs[at + len(later) :])

    return pl.pallas_call(
        body,
        out_shape=outs,
        in_specs=[SCALARS] * scalars + [ANYWHERE] * held + [pl.BlockSpec(memory_space=pl.ANY)] * (far + len(later)),
        out_specs=jax.tree.map(lambda _: out_spec, outs),
        scratch_shapes=scratch,
        compiler_params=pltpu.CompilerParams(vmem_limit_bytes=VMEM_LIMIT),
        cost_estimate=pl.CostEstimate(flops=flops, bytes_accessed=1024, transcendentals=0),
    )(*operands, *later)


def pick_kernel(where_ref, own, one, two, three, up, down):
    z = where_ref[0]
    for at in range(ROW):

        @pl.when(z == at)
        def _():
            ring = (own, one, two, three)
            for out, blocks in ((up, (2, 3)), (down, (0, 1))):
                for at_out, block in enumerate(blocks):
                    out[at_out] = ring[(block - at) % ROW][:2]


def pick_one_kernel(where_ref, own, one, two, three, out):
    z = where_ref[0]
    for at in range(ROW):

        @pl.when(z == at)
        def _():
            ring = (own, one, two, three)
            base = 2 if at < 2 else 0
            out[0] = ring[(base - at) % ROW][...]
            out[1] = ring[(base + 1 - at) % ROW][...]


def spot(index):
    return pl.ds(pl.multiple_of(index * TILE, TILE), TILE)


def spread(where_ref, place_ref, ring, targets):
    z = where_ref[0]
    for j in range(ROW):
        block = lax.rem(z + j, ROW)
        for i in range(4):
            at = spot((block // 2) * SLAB + place_ref[0, SLAB + block * 4 + i])
            for target, piece in zip(targets, ring[j]):
                target[at, :] = piece[i * TILE : (i + 1) * TILE, :]


def softmax_rows(q, parts, valid, scale):
    scores = [
        lax.dot_general(q, keys, (((1,), (1,)), ((), ())), preferred_element_type=jnp.float32) for keys, _ in parts
    ]
    tops = [jnp.max(s, axis=-1, keepdims=True) for s in scores]
    tops[-1] = jnp.where(valid, tops[-1], NEG)
    top = functools.reduce(jnp.maximum, tops)
    total, summed = 0.0, 0.0
    for at, (s, (_, values)) in enumerate(zip(scores, parts)):
        weights = jnp.exp2((s - top) * (scale * LOG2E))
        part_total = jnp.sum(weights, axis=-1, keepdims=True)
        part_sum = jnp.dot(weights.astype(jnp.bfloat16), values, preferred_element_type=jnp.float32)
        if at == len(parts) - 1:
            part_total = jnp.where(valid, part_total, 0.0)
            part_sum = jnp.where(valid, part_sum, 0.0)
        total, summed = total + part_total, summed + part_sum
    return summed / total


WINDOW = ((0, 512), (0, 768), (256, 1024), (512, 1024))


def piece_scores(q, keys):
    return lax.dot_general(q, keys, (((1,), (1,)), ((), ())), preferred_element_type=jnp.float32)


def near_kernel(where_ref, place_ref, kvq0, kvq1, kvq2, kvq3, qs, acc, stats, ks, vs):
    factor = ks.shape[-1] ** -0.5 * LOG2E
    ring = [(kvq.at[0], kvq.at[1], kvq.at[2]) for kvq in (kvq0, kvq1, kvq2, kvq3)]
    spread(where_ref, place_ref, ring, (ks, vs, qs))
    lane = lax.broadcasted_iota(jnp.int32, (256, 128), 1)
    for s in range(2):
        for column, (low, high) in enumerate(WINDOW):
            rows = slice(s * 1024 + column * 256, s * 1024 + column * 256 + 256)
            q = qs[rows, :]
            pieces = [slice(t * 1024 + low, t * 1024 + high) for t in range(2)]
            scores = [piece_scores(q, ks[piece, :]) for piece in pieces]
            top = functools.reduce(jnp.maximum, [jnp.max(p, axis=-1, keepdims=True) for p in scores])
            total, summed = 0.0, 0.0
            for piece, score in zip(pieces, scores):
                weights = jnp.exp2((score - top) * factor)
                total = total + jnp.sum(weights, axis=-1, keepdims=True)
                summed = summed + jnp.dot(
                    weights.astype(jnp.bfloat16), vs[piece, :], preferred_element_type=jnp.float32
                )
            acc[rows, :] = summed
            stats[rows, :] = jnp.where(lane == 0, top, total)


def halo_kernel(where_ref, place_ref, qs, acc, stats, up, down, o0, o1, o2, o3, ks, vs, os):
    factor = qs.shape[-1] ** -0.5 * LOG2E
    for side, first, slab in ((up, 0, 0), (down, 24, 1)):
        for b in range(2):
            for i in range(4):
                at = spot(slab * SLAB + place_ref[0, first + b * 4 + i])
                rows = slice(i * TILE, (i + 1) * TILE)
                ks[at, :] = side[b, 0, rows, :]
                vs[at, :] = side[b, 1, rows, :]
    for s in range(2):
        valid = where_ref[1 + s] > 0
        for column, (low, high) in enumerate(WINDOW):
            rows = slice(s * 1024 + column * 256, s * 1024 + column * 256 + 256)
            piece = slice(s * 1024 + low, s * 1024 + high)
            score = piece_scores(qs[rows, :], ks[piece, :])
            before = stats[rows, :]
            top_before, total_before = before[:, 0:1], before[:, 1:2]
            top = jnp.maximum(top_before, jnp.where(valid, jnp.max(score, axis=-1, keepdims=True), NEG))
            weights = jnp.exp2((score - top) * factor)
            total = jnp.where(valid, jnp.sum(weights, axis=-1, keepdims=True), 0.0)
            summed = jnp.dot(weights.astype(jnp.bfloat16), vs[piece, :], preferred_element_type=jnp.float32)
            summed = jnp.where(valid, summed, 0.0)
            shrink = jnp.exp2((top_before - top) * factor)
            total = total + total_before * shrink
            os[rows, :] = ((summed + acc[rows, :] * shrink) / total).astype(jnp.bfloat16)
    z = where_ref[0]
    for j, out in enumerate((o0, o1, o2, o3)):
        block = lax.rem(z + j, ROW)
        for i in range(4):
            at = spot((block // 2) * SLAB + place_ref[0, SLAB + block * 4 + i])
            out[i * TILE : (i + 1) * TILE, :] = os[at, :]


def rest_kernel(where_ref, place_ref, kv0, kv1, kv2, kv3, q, halo, out, ks, vs):
    scale = q.shape[-1] ** -0.5
    z = where_ref[0]
    ring = [(kv.at[0], kv.at[1]) for kv in (kv0, kv1, kv2, kv3)]
    spread(where_ref, place_ref, ring, (ks.at[0:2048], vs.at[0:2048]))
    first = jnp.where(z < 2, 0, 24)
    valid = jnp.where(z < 2, where_ref[1], where_ref[2]) > 0
    for b in range(2):
        for i in range(4):
            at = spot(2 * SLAB + place_ref[0, first + b * 4 + i])
            rows = slice(i * TILE, (i + 1) * TILE)
            ks[at, :] = halo[b, 0, rows, :]
            vs[at, :] = halo[b, 1, rows, :]

    @pl.loop(0, 4)
    def _(i):
        column = place_ref[0, SLAB + z * 4 + i] // 2
        low = jnp.maximum(column - 1, 0) * 256
        here = spot(i)
        edge = (column == 0) | (column == 3)

        def work(width):
            parts = []
            for t in range(3):
                at = pl.ds(pl.multiple_of(t * 1024 + low, 256), width)
                parts.append((ks[at, :], vs[at, :]))
            out[here, :] = softmax_rows(q[here, :], parts, valid, scale).astype(jnp.bfloat16)

        @pl.when(edge)
        def _():
            work(512)

        @pl.when(jnp.logical_not(edge))
        def _():
            work(768)


def place_heads(z, ring, wide, base):
    for j in range(ROW):
        head = lax.rem(z + j, ROW)
        at = pl.multiple_of(base + head * TILE, TILE)
        wide[:, pl.ds(at, TILE)] = ring[j]
    wide[:, base + ROW * TILE : base + (ROW + 1) * TILE] = ring[ROW]


STRIP = 256


def strips(width):
    return [slice(n, n + STRIP) for n in range(0, width, STRIP)]


def project_kernel(where_ref, m0, w0, m1, w1, out, wide):
    z = where_ref[0]
    place_heads(z, m0, wide, 0)
    place_heads(z, m1, wide, 640)
    for at in strips(out.shape[1]):
        out[:, at] = jnp.dot(wide[:, :640], w0[:, at], preferred_element_type=jnp.float32) + jnp.dot(
            wide[:, 640:], w1[:, at], preferred_element_type=jnp.float32
        )


def finish_kernel(where_ref, m0, w0, m1, w1, before, out, wide, rounded, sem):
    z = where_ref[0]
    place_heads(z, m0, wide, 0)
    place_heads(z, m1, wide, 640)
    copies = []
    for n, at in enumerate(strips(out.shape[1])):
        part = before[:, at] + jnp.dot(wide[:, :640], w0[:, at], preferred_element_type=jnp.float32)
        part = part + jnp.dot(wide[:, 640:], w1[:, at], preferred_element_type=jnp.float32)
        rounded[:, at] = part.astype(rounded.dtype)
        copies.append(pltpu.make_async_copy(rounded.at[:, at], out.at[:, at], sem.at[n]))
        copies[-1].start()
    for copy in copies:
        copy.wait()


def fetch(copies):
    for copy in copies:
        copy.start()
    for copy in copies:
        copy.wait()


def theirs_kernel(where_ref, weight, out, sem):
    heads, _, width = weight.shape
    at = pl.ds(pl.multiple_of((1 - where_ref[4]) * (width // 2), TILE), width // 2)
    fetch([pltpu.make_async_copy(weight.at[h, :, at], out.at[spot(h), :], sem.at[h]) for h in range(heads)])


def own_halves_kernel(where_ref, weight, mine, other, sem):
    heads, _, width = weight.shape
    cols, c = width // 4, where_ref[5]
    copies = []
    for k, (out, core) in enumerate(((mine, c), (other, 1 - c))):
        at = pl.ds(pl.multiple_of((where_ref[4] * 2 + core) * cols, TILE), cols)
        copies += [
            pltpu.make_async_copy(weight.at[h, :, at], out.at[spot(h), :], sem.at[k * heads + h]) for h in range(heads)
        ]
    fetch(copies)


def far_halves_kernel(where_ref, weight, mine, other, sem):
    cols, c = weight.shape[1] // 2, where_ref[5]
    copies = []
    for k, (out, core) in enumerate(((mine, c), (other, 1 - c))):
        at = pl.ds(pl.multiple_of(core * cols, TILE), cols)
        copies.append(pltpu.make_async_copy(weight.at[:, at], out, sem.at[k]))
    fetch(copies)


def local(queries, key_rows, value_rows, out_weight, tile_mask):
    tok, heads, size = queries.shape
    rows = lax.axis_size("seq") // ROW
    seq, head = lax.axis_index("seq"), lax.axis_index("head")
    row, z = seq // ROW, seq % ROW
    yl, c = head // 2, head % 2
    bf = jnp.bfloat16
    wide_cols = out_weight.shape[-1] // 2
    cols = wide_cols // 2
    row_tok = ROW * tok
    block = jax.ShapeDtypeStruct((tok, size), bf)
    halo = jax.ShapeDtypeStruct((2, 2, tok, size), bf)

    def ring_slices(array):
        return [lax.dynamic_index_in_dim(array, (z + j) % ROW, 0, keepdims=False) for j in range(ROW)]

    def sibling(piece):
        return send(piece, rows, lambda r, z, yl, c: (r, z, yl, 1 - c))

    def y_pair(piece):
        return send(piece, rows, lambda r, z, yl, c: (r, z, 1 - yl, c))

    with jax.named_scope("lay_out"):
        kvq = jnp.stack([key_rows, value_rows, queries]).transpose(2, 0, 1, 3)
        own, *out = [lax.dynamic_index_in_dim(kvq, (z + j) % ROW, 0, keepdims=False) for j in range(ROW)]
        kv_rest, q_rest = kvq[ROW, :2], kvq[ROW, 2]
    with jax.named_scope("head_z"):
        ring = along_z(out, rows)

    with jax.named_scope("weights_y"):
        where = jnp.stack([z, row > 0, row < rows - 1, row * 2 * SLAB - SLAB, yl, c]).astype(jnp.int32)
        theirs = call(
            theirs_kernel,
            jax.ShapeDtypeStruct((heads * size, wide_cols), bf),
            [pltpu.SemaphoreType.DMA((heads,))],
            [where, out_weight],
            1,
            later=out[:1],
            far=1,
            flops=8000000000,
        )

        def y_step(r, z, yl, c):
            yh, x = r // ROW, r % ROW
            y = (yh * 2 + yl + (1 if c == 0 else -1)) % 4
            return ((y // 2) * ROW + x, z, y % 2, c)

        w_far = send(theirs, rows, y_step)

    with jax.named_scope("pick"):
        to_next, to_prev = call(pick_kernel, (halo, halo), [], [where, own, *ring], 1)
    with jax.named_scope("head_x"):
        from_prev = send(to_next, rows, lambda r, z, yl, c: (r + 1, z, yl, c) if r + 1 < rows else None)
        from_next = send(to_prev, rows, lambda r, z, yl, c: (r - 1, z, yl, c) if r > 0 else None)
    with jax.named_scope("places"):
        place, kv_rest = call(
            places_kernel,
            (jax.ShapeDtypeStruct((1, 4 * SLAB), jnp.int32), jax.ShapeDtypeStruct((2, tok, size), bf)),
            [],
            [where, tile_mask, kv_rest],
            1,
            later=[to_next],
            flops=8000000000,
        )
    with jax.named_scope("rest_z"):
        rest_in = along_z([kv_rest] * 3, rows)
    with jax.named_scope("rest_pick"):
        to_rest = call(pick_one_kernel, halo, [], [where, kv_rest, *rest_in], 1)
    with jax.named_scope("rest_x"):

        def rest_step(r, z, yl, c):
            to = r + 1 if z < 2 else r - 1
            return (to, z, yl, c) if 0 <= to < rows else None

        rest_halo = send(to_rest, rows, rest_step)
    with jax.named_scope("near_attention"):
        qs, acc, stats = call(
            near_kernel,
            (
                jax.ShapeDtypeStruct((row_tok, size), bf),
                jax.ShapeDtypeStruct((row_tok, size), jnp.float32),
                jax.ShapeDtypeStruct((row_tok, size), jnp.float32),
            ),
            [pltpu.VMEM((row_tok, size), bf), pltpu.VMEM((row_tok, size), bf)],
            [where, place, own, *ring],
            2,
            flops=8000000000,
        )
    with jax.named_scope("halo_attention"):
        o_own, *o_out = call(
            halo_kernel,
            (block,) * 4,
            [pltpu.VMEM((row_tok, size), bf)] * 3,
            [where, place, qs, acc, stats, from_prev, from_next],
            2,
            later=[to_rest],
            flops=1000000000,
        )
    with jax.named_scope("attended_z"):
        o_in = along_z(o_out, rows)
    half = jax.ShapeDtypeStruct((heads * size, cols), bf)
    with jax.named_scope("weights_core"):
        w_own, w_own_other = call(
            own_halves_kernel,
            (half, half),
            [pltpu.SemaphoreType.DMA((2 * heads,))],
            [where, out_weight],
            1,
            later=[o_own],
            far=1,
        )
        w_sib = sibling(w_own_other)
    with jax.named_scope("rest_attention"):
        o_rest = call(
            rest_kernel,
            block,
            [pltpu.VMEM((6 * tok, size), bf), pltpu.VMEM((6 * tok, size), bf)],
            [where, place, kv_rest, *rest_in, q_rest, rest_halo],
            2,
            later=[o_own],
            flops=3000000000,
        )
    with jax.named_scope("weights_far_core"):
        w_y, w_y_other = call(
            far_halves_kernel,
            (half, half),
            [pltpu.SemaphoreType.DMA((2,))],
            [where, w_far],
            1,
            later=[o_rest],
            far=1,
            flops=1000000000,
        )
        w_y_sib = sibling(w_y_other)
    mine = jnp.stack([o_own, *o_in, o_rest])
    with jax.named_scope("attended_y"):
        far = y_pair(mine)
    with jax.named_scope("attended_core"):
        mine_sib = sibling(mine)
    wide = pltpu.VMEM((tok, 2 * heads * size), bf)
    with jax.named_scope("project"):
        near = call(
            project_kernel,
            jax.ShapeDtypeStruct((tok, cols), jnp.float32),
            [wide],
            [where, mine, w_own, mine_sib, w_sib],
            1,
            flops=10000000000,
        )
    with jax.named_scope("far_core"):
        near, far = together(near, far)
        far_sib = sibling(far)
    with jax.named_scope("finish"):
        return call(
            finish_kernel,
            jax.ShapeDtypeStruct((tok, cols), bf),
            [wide, pltpu.VMEM((tok, cols), bf), pltpu.SemaphoreType.DMA((cols // STRIP,))],
            [where, far, w_y, far_sib, w_y_sib, near],
            1,
            out_spec=pl.BlockSpec(memory_space=pl.ANY),
        )


def solution(mesh):
    placed = (
        P("seq", "head", None),
        P("seq", "head", None),
        P("seq", "head", None),
        P("head", None, None),
        P(),
    )
    return jax.shard_map(local, mesh=mesh, in_specs=placed, out_specs=P("seq", "head"), check_vma=False)
```

```python
import functools

import jax
import jax.numpy as jnp
from jax import lax
from jax.experimental import pallas as pl
from jax.experimental.pallas import tpu as pltpu
from jax.sharding import PartitionSpec as P

TILE = 128
SLAB = 8
ROW = 4
NEG = -1e30
LOG2E = 1.4426950408889634
AXES = ("seq", "head")
VMEM_LIMIT = 16 * 1024 * 1024


def route(rows, target):
    pairs = []
    for row in range(rows):
        for z in range(ROW):
            for yl in range(2):
                for c in range(2):
                    to = target(row, z, yl, c)
                    if to is not None:
                        dst = ((to[0] * ROW + to[1]) * 2 + to[2]) * 2 + to[3]
                        pairs.append((((row * ROW + z) * 2 + yl) * 2 + c, dst))
    return pairs


def send(block, rows, target):
    return lax.ppermute(block, AXES, route(rows, target))


def along_z(blocks, rows):
    plus, two, minus = (
        send(blocks[j - 1], rows, lambda r, z, yl, c, j=j: (r, (z + j) % ROW, yl, c)) for j in (1, 2, 3)
    )
    return [minus, two, plus]


def together(*arrays):
    return lax.optimization_barrier(arrays)


def places_kernel(where_ref, mask_ref, rest_ref, out, rest_out):
    rest_out[...] = rest_ref[...]
    count = mask_ref.shape[0]
    start = where_ref[3]
    pick = lax.broadcasted_iota(jnp.int32, (4 * SLAB, count), 1) - lax.broadcasted_iota(jnp.int32, (4 * SLAB, count), 0)
    pick = jnp.where(pick == start, 1.0, 0.0)
    rows = jnp.dot(pick, (mask_ref[...] > 0).astype(jnp.float32), preferred_element_type=jnp.float32)
    near = lax.dot_general(rows, pick, (((1,), (1,)), ((), ())), preferred_element_type=jnp.float32)
    live = jnp.where(near > 0.5, 1, 0)
    shape = live.shape
    down = lax.broadcasted_iota(jnp.int32, shape, 0)
    across = lax.broadcasted_iota(jnp.int32, shape, 1)
    same_slab = (down // SLAB) == (across // SLAB)
    inside = jnp.where(same_slab, live, 0)
    lane = across[:1]
    degree = (jnp.sum(inside, axis=0, keepdims=True), jnp.sum(inside, axis=1, keepdims=True))
    edge_row = degree[0] == 4

    def beside(reference):
        return (
            jnp.sum(jnp.where(down == reference, live, 0), axis=0, keepdims=True),
            jnp.sum(jnp.where(across == reference, live, 0), axis=1, keepdims=True),
        )

    first = jnp.min(jnp.where(edge_row & (lane // SLAB == 1), lane, 4 * SLAB), axis=1, keepdims=True)
    one = beside(first)
    second = jnp.min(jnp.where(edge_row & (lane // SLAB == 2) & (one[0] > 0), lane, 4 * SLAB), axis=1, keepdims=True)
    two = beside(second)
    column = []
    for at, index in ((0, lane), (1, down[:, :1])):
        side = jnp.where(index < 3 * SLAB, one[at], two[at]) > 0
        middle = jnp.where(degree[at] == 4, 0, 1)
        column.append(jnp.where(side, middle, 3 - middle))
    twin = same_slab & (column[0] == column[1]) & (down < across)
    place = column[0] * 2 + jnp.sum(jnp.where(twin, 1, 0), axis=0, keepdims=True)
    place = jnp.where(degree[0] == 0, lane % SLAB, place)
    out[...] = jnp.clip(place, 0, SLAB - 1)


ANYWHERE = pl.BlockSpec(memory_space=pltpu.VMEM)
SCALARS = pl.BlockSpec(memory_space=pltpu.SMEM)


def call(kernel, outs, scratch, operands, scalars, flops=1024, later=(), far=0, out_spec=ANYWHERE):
    held = len(operands) - scalars - far

    def body(*refs):
        at = len(operands)
        kernel(*refs[:at], *refs[at + len(later) :])

    return pl.pallas_call(
        body,
        out_shape=outs,
        in_specs=[SCALARS] * scalars + [ANYWHERE] * held + [pl.BlockSpec(memory_space=pl.ANY)] * (far + len(later)),
        out_specs=jax.tree.map(lambda _: out_spec, outs),
        scratch_shapes=scratch,
        compiler_params=pltpu.CompilerParams(vmem_limit_bytes=VMEM_LIMIT),
        cost_estimate=pl.CostEstimate(flops=flops, bytes_accessed=1024, transcendentals=0),
    )(*operands, *later)


def pick_kernel(where_ref, own, one, two, three, up, down):
    z = where_ref[0]
    for at in range(ROW):

        @pl.when(z == at)
        def _():
            ring = (own, one, two, three)
            for out, blocks in ((up, (2, 3)), (down, (0, 1))):
                for at_out, block in enumerate(blocks):
                    out[at_out] = ring[(block - at) % ROW][:2]


def pick_one_kernel(where_ref, own, one, two, three, out):
    z = where_ref[0]
    for at in range(ROW):

        @pl.when(z == at)
        def _():
            ring = (own, one, two, three)
            base = 2 if at < 2 else 0
            out[0] = ring[(base - at) % ROW][...]
            out[1] = ring[(base + 1 - at) % ROW][...]


def spot(index):
    return pl.ds(pl.multiple_of(index * TILE, TILE), TILE)


def spread(where_ref, place_ref, ring, targets):
    z = where_ref[0]
    for j in range(ROW):
        block = lax.rem(z + j, ROW)
        for i in range(4):
            at = spot((block // 2) * SLAB + place_ref[0, SLAB + block * 4 + i])
            for target, piece in zip(targets, ring[j]):
                target[at, :] = piece[i * TILE : (i + 1) * TILE, :]


def softmax_rows(q, parts, valid, scale):
    scores = [
        lax.dot_general(q, keys, (((1,), (1,)), ((), ())), preferred_element_type=jnp.float32) for keys, _ in parts
    ]
    tops = [jnp.max(s, axis=-1, keepdims=True) for s in scores]
    tops[-1] = jnp.where(valid, tops[-1], NEG)
    top = functools.reduce(jnp.maximum, tops)
    total, summed = 0.0, 0.0
    for at, (s, (_, values)) in enumerate(zip(scores, parts)):
        weights = jnp.exp2((s - top) * (scale * LOG2E))
        part_total = jnp.sum(weights, axis=-1, keepdims=True)
        part_sum = jnp.dot(weights.astype(jnp.bfloat16), values, preferred_element_type=jnp.float32)
        if at == len(parts) - 1:
            part_total = jnp.where(valid, part_total, 0.0)
            part_sum = jnp.where(valid, part_sum, 0.0)
        total, summed = total + part_total, summed + part_sum
    return summed / total


WINDOW = ((0, 512), (0, 768), (256, 1024), (512, 1024))


def piece_scores(q, keys):
    return lax.dot_general(q, keys, (((1,), (1,)), ((), ())), preferred_element_type=jnp.float32)


def near_kernel(where_ref, place_ref, kvq0, kvq1, kvq2, kvq3, qs, acc, stats, ks, vs):
    factor = ks.shape[-1] ** -0.5 * LOG2E
    ring = [(kvq.at[0], kvq.at[1], kvq.at[2]) for kvq in (kvq0, kvq1, kvq2, kvq3)]
    spread(where_ref, place_ref, ring, (ks, vs, qs))
    lane = lax.broadcasted_iota(jnp.int32, (256, 128), 1)
    for s in range(2):
        for column, (low, high) in enumerate(WINDOW):
            rows = slice(s * 1024 + column * 256, s * 1024 + column * 256 + 256)
            q = qs[rows, :]
            pieces = [slice(t * 1024 + low, t * 1024 + high) for t in range(2)]
            scores = [piece_scores(q, ks[piece, :]) for piece in pieces]
            top = functools.reduce(jnp.maximum, [jnp.max(p, axis=-1, keepdims=True) for p in scores])
            total, summed = 0.0, 0.0
            for piece, score in zip(pieces, scores):
                weights = jnp.exp2((score - top) * factor)
                total = total + jnp.sum(weights, axis=-1, keepdims=True)
                summed = summed + jnp.dot(
                    weights.astype(jnp.bfloat16), vs[piece, :], preferred_element_type=jnp.float32
                )
            acc[rows, :] = summed
            stats[rows, :] = jnp.where(lane == 0, top, total)


def halo_kernel(where_ref, place_ref, qs, acc, stats, up, down, o0, o1, o2, o3, ks, vs, os):
    factor = qs.shape[-1] ** -0.5 * LOG2E
    for side, first, slab in ((up, 0, 0), (down, 24, 1)):
        for b in range(2):
            for i in range(4):
                at = spot(slab * SLAB + place_ref[0, first + b * 4 + i])
                rows = slice(i * TILE, (i + 1) * TILE)
                ks[at, :] = side[b, 0, rows, :]
                vs[at, :] = side[b, 1, rows, :]
    for s in range(2):
        valid = where_ref[1 + s] > 0
        for column, (low, high) in enumerate(WINDOW):
            rows = slice(s * 1024 + column * 256, s * 1024 + column * 256 + 256)
            piece = slice(s * 1024 + low, s * 1024 + high)
            score = piece_scores(qs[rows, :], ks[piece, :])
            before = stats[rows, :]
            top_before, total_before = before[:, 0:1], before[:, 1:2]
            top = jnp.maximum(top_before, jnp.where(valid, jnp.max(score, axis=-1, keepdims=True), NEG))
            weights = jnp.exp2((score - top) * factor)
            total = jnp.where(valid, jnp.sum(weights, axis=-1, keepdims=True), 0.0)
            summed = jnp.dot(weights.astype(jnp.bfloat16), vs[piece, :], preferred_element_type=jnp.float32)
            summed = jnp.where(valid, summed, 0.0)
            shrink = jnp.exp2((top_before - top) * factor)
            total = total + total_before * shrink
            os[rows, :] = ((summed + acc[rows, :] * shrink) / total).astype(jnp.bfloat16)
    z = where_ref[0]
    for j, out in enumerate((o0, o1, o2, o3)):
        block = lax.rem(z + j, ROW)
        for i in range(4):
            at = spot((block // 2) * SLAB + place_ref[0, SLAB + block * 4 + i])
            out[i * TILE : (i + 1) * TILE, :] = os[at, :]


def rest_kernel(where_ref, place_ref, kv0, kv1, kv2, kv3, q, halo, out, ks, vs):
    scale = q.shape[-1] ** -0.5
    z = where_ref[0]
    ring = [(kv.at[0], kv.at[1]) for kv in (kv0, kv1, kv2, kv3)]
    spread(where_ref, place_ref, ring, (ks.at[0:2048], vs.at[0:2048]))
    first = jnp.where(z < 2, 0, 24)
    valid = jnp.where(z < 2, where_ref[1], where_ref[2]) > 0
    for b in range(2):
        for i in range(4):
            at = spot(2 * SLAB + place_ref[0, first + b * 4 + i])
            rows = slice(i * TILE, (i + 1) * TILE)
            ks[at, :] = halo[b, 0, rows, :]
            vs[at, :] = halo[b, 1, rows, :]

    for i in range(4):
        column = place_ref[0, SLAB + z * 4 + i] // 2
        low = jnp.maximum(column - 1, 0) * 256
        here = slice(i * TILE, (i + 1) * TILE)
        edge = (column == 0) | (column == 3)

        def work(width):
            parts = []
            for t in range(3):
                at = pl.ds(pl.multiple_of(t * 1024 + low, 256), width)
                parts.append((ks[at, :], vs[at, :]))
            out[here, :] = softmax_rows(q[here, :], parts, valid, scale).astype(jnp.bfloat16)

        @pl.when(edge)
        def _():
            work(512)

        @pl.when(jnp.logical_not(edge))
        def _():
            work(768)


def place_heads(z, ring, wide, base):
    for j in range(ROW):
        head = lax.rem(z + j, ROW)
        at = pl.multiple_of(base + head * TILE, TILE)
        wide[:, pl.ds(at, TILE)] = ring[j]
    wide[:, base + ROW * TILE : base + (ROW + 1) * TILE] = ring[ROW]


STRIP = 256


def strips(width):
    return [slice(n, n + STRIP) for n in range(0, width, STRIP)]


def project_kernel(where_ref, m0, w0, m1, w1, out, wide):
    z = where_ref[0]
    place_heads(z, m0, wide, 0)
    place_heads(z, m1, wide, 640)
    for at in strips(out.shape[1]):
        out[:, at] = jnp.dot(wide[:, :640], w0[:, at], preferred_element_type=jnp.float32) + jnp.dot(
            wide[:, 640:], w1[:, at], preferred_element_type=jnp.float32
        )


def finish_kernel(where_ref, m0, w0, m1, w1, before, out, wide, rounded, sem):
    z = where_ref[0]
    place_heads(z, m0, wide, 0)
    place_heads(z, m1, wide, 640)
    copies = []
    for n, at in enumerate(strips(out.shape[1])):
        part = before[:, at] + jnp.dot(wide[:, :640], w0[:, at], preferred_element_type=jnp.float32)
        part = part + jnp.dot(wide[:, 640:], w1[:, at], preferred_element_type=jnp.float32)
        rounded[:, at] = part.astype(rounded.dtype)
        copies.append(pltpu.make_async_copy(rounded.at[:, at], out.at[:, at], sem.at[n]))
        copies[-1].start()
    for copy in copies:
        copy.wait()


def fetch(copies):
    for copy in copies:
        copy.start()
    for copy in copies:
        copy.wait()


def theirs_kernel(where_ref, weight, out, sem):
    heads, _, width = weight.shape
    at = pl.ds(pl.multiple_of((1 - where_ref[4]) * (width // 2), TILE), width // 2)
    fetch([pltpu.make_async_copy(weight.at[h, :, at], out.at[spot(h), :], sem.at[h]) for h in range(heads)])


def own_halves_kernel(where_ref, weight, mine, other, sem):
    heads, _, width = weight.shape
    cols, c = width // 4, where_ref[5]
    copies = []
    for k, (out, core) in enumerate(((mine, c), (other, 1 - c))):
        at = pl.ds(pl.multiple_of((where_ref[4] * 2 + core) * cols, TILE), cols)
        copies += [
            pltpu.make_async_copy(weight.at[h, :, at], out.at[spot(h), :], sem.at[k * heads + h]) for h in range(heads)
        ]
    fetch(copies)


def far_halves_kernel(where_ref, weight, mine, other, sem):
    cols, c = weight.shape[1] // 2, where_ref[5]
    copies = []
    for k, (out, core) in enumerate(((mine, c), (other, 1 - c))):
        at = pl.ds(pl.multiple_of(core * cols, TILE), cols)
        copies.append(pltpu.make_async_copy(weight.at[:, at], out, sem.at[k]))
    fetch(copies)


def local(queries, key_rows, value_rows, out_weight, tile_mask):
    tok, heads, size = queries.shape
    rows = lax.axis_size("seq") // ROW
    seq, head = lax.axis_index("seq"), lax.axis_index("head")
    row, z = seq // ROW, seq % ROW
    yl, c = head // 2, head % 2
    bf = jnp.bfloat16
    wide_cols = out_weight.shape[-1] // 2
    cols = wide_cols // 2
    row_tok = ROW * tok
    block = jax.ShapeDtypeStruct((tok, size), bf)
    halo = jax.ShapeDtypeStruct((2, 2, tok, size), bf)

    def ring_slices(array):
        return [lax.dynamic_index_in_dim(array, (z + j) % ROW, 0, keepdims=False) for j in range(ROW)]

    def sibling(piece):
        return send(piece, rows, lambda r, z, yl, c: (r, z, yl, 1 - c))

    def y_pair(piece):
        return send(piece, rows, lambda r, z, yl, c: (r, z, 1 - yl, c))

    with jax.named_scope("lay_out"):
        kvq = jnp.stack([key_rows, value_rows, queries]).transpose(2, 0, 1, 3)
        own, *out = [lax.dynamic_index_in_dim(kvq, (z + j) % ROW, 0, keepdims=False) for j in range(ROW)]
        kv_rest, q_rest = kvq[ROW, :2], kvq[ROW, 2]
    with jax.named_scope("head_z"):
        ring = along_z(out, rows)

    with jax.named_scope("weights_y"):
        where = jnp.stack([z, row > 0, row < rows - 1, row * 2 * SLAB - SLAB, yl, c]).astype(jnp.int32)
        theirs = call(
            theirs_kernel,
            jax.ShapeDtypeStruct((heads * size, wide_cols), bf),
            [pltpu.SemaphoreType.DMA((heads,))],
            [where, out_weight],
            1,
            later=out[:1],
            far=1,
            flops=8000000000,
        )

        def y_step(r, z, yl, c):
            yh, x = r // ROW, r % ROW
            y = (yh * 2 + yl + (1 if c == 0 else -1)) % 4
            return ((y // 2) * ROW + x, z, y % 2, c)

        w_far = send(theirs, rows, y_step)

    with jax.named_scope("pick"):
        to_next, to_prev = call(pick_kernel, (halo, halo), [], [where, own, *ring], 1)
    with jax.named_scope("head_x"):
        from_prev = send(to_next, rows, lambda r, z, yl, c: (r + 1, z, yl, c) if r + 1 < rows else None)
        from_next = send(to_prev, rows, lambda r, z, yl, c: (r - 1, z, yl, c) if r > 0 else None)
    with jax.named_scope("places"):
        place, kv_rest = call(
            places_kernel,
            (jax.ShapeDtypeStruct((1, 4 * SLAB), jnp.int32), jax.ShapeDtypeStruct((2, tok, size), bf)),
            [],
            [where, tile_mask, kv_rest],
            1,
            later=[to_next],
            flops=8000000000,
        )
    with jax.named_scope("rest_z"):
        rest_in = along_z([kv_rest] * 3, rows)
    with jax.named_scope("rest_pick"):
        to_rest = call(pick_one_kernel, halo, [], [where, kv_rest, *rest_in], 1)
    with jax.named_scope("rest_x"):

        def rest_step(r, z, yl, c):
            to = r + 1 if z < 2 else r - 1
            return (to, z, yl, c) if 0 <= to < rows else None

        rest_halo = send(to_rest, rows, rest_step)
    with jax.named_scope("near_attention"):
        qs, acc, stats = call(
            near_kernel,
            (
                jax.ShapeDtypeStruct((row_tok, size), bf),
                jax.ShapeDtypeStruct((row_tok, size), jnp.float32),
                jax.ShapeDtypeStruct((row_tok, size), jnp.float32),
            ),
            [pltpu.VMEM((row_tok, size), bf), pltpu.VMEM((row_tok, size), bf)],
            [where, place, own, *ring],
            2,
            flops=8000000000,
        )
    with jax.named_scope("halo_attention"):
        o_own, *o_out = call(
            halo_kernel,
            (block,) * 4,
            [pltpu.VMEM((row_tok, size), bf)] * 3,
            [where, place, qs, acc, stats, from_prev, from_next],
            2,
            later=[to_rest],
            flops=1000000000,
        )
    with jax.named_scope("attended_z"):
        o_in = along_z(o_out, rows)
    half = jax.ShapeDtypeStruct((heads * size, cols), bf)
    with jax.named_scope("weights_core"):
        w_own, w_own_other = call(
            own_halves_kernel,
            (half, half),
            [pltpu.SemaphoreType.DMA((2 * heads,))],
            [where, out_weight],
            1,
            later=[o_own],
            far=1,
        )
        w_sib = sibling(w_own_other)
    with jax.named_scope("rest_attention"):
        o_rest = call(
            rest_kernel,
            block,
            [pltpu.VMEM((6 * tok, size), bf), pltpu.VMEM((6 * tok, size), bf)],
            [where, place, kv_rest, *rest_in, q_rest, rest_halo],
            2,
            later=[o_own],
            flops=3000000000,
        )
    with jax.named_scope("weights_far_core"):
        w_y, w_y_other = call(
            far_halves_kernel,
            (half, half),
            [pltpu.SemaphoreType.DMA((2,))],
            [where, w_far],
            1,
            later=[o_rest],
            far=1,
            flops=1000000000,
        )
        w_y_sib = sibling(w_y_other)
    mine = jnp.stack([o_own, *o_in, o_rest])
    with jax.named_scope("attended_y"):
        far = y_pair(mine)
    with jax.named_scope("attended_core"):
        mine_sib = sibling(mine)
    wide = pltpu.VMEM((tok, 2 * heads * size), bf)
    with jax.named_scope("project"):
        near = call(
            project_kernel,
            jax.ShapeDtypeStruct((tok, cols), jnp.float32),
            [wide],
            [where, mine, w_own, mine_sib, w_sib],
            1,
            flops=10000000000,
        )
    with jax.named_scope("far_core"):
        near, far = together(near, far)
        far_sib = sibling(far)
    with jax.named_scope("finish"):
        return call(
            finish_kernel,
            jax.ShapeDtypeStruct((tok, cols), bf),
            [wide, pltpu.VMEM((tok, cols), bf), pltpu.SemaphoreType.DMA((cols // STRIP,))],
            [where, far, w_y, far_sib, w_y_sib, near],
            1,
            out_spec=pl.BlockSpec(memory_space=pl.ANY),
        )


def solution(mesh):
    placed = (
        P("seq", "head", None),
        P("seq", "head", None),
        P("seq", "head", None),
        P("head", None, None),
        P(),
    )
    return jax.shard_map(local, mesh=mesh, in_specs=placed, out_specs=P("seq", "head"), check_vma=False)
```
